32 devices in a mesh: groups: 2 (over y), seq: 4 (over x, core), shard: 4 (over z).
Axes of the slice: x: 2, y: 2, z: 4, core: 2. Of those that a mesh axis runs over, the one named last changes fastest.
Arguments:
- qkv_img: bfloat16 [3, 8, 512, 2048], P(None, ('groups', 'shard'), 'seq'), parts along dimension 1, may hold values from -12 to 12
- qkv_txt: bfloat16 [3, 8, 64, 2048], P(None, ('groups', 'shard'), 'seq'), parts along dimension 1, may hold values from -8 to 8
- grad_img: bfloat16 [8, 512, 3072], P(('groups', 'shard'), 'seq'), parts along dimension 0, may hold values from -24 to 24
- grad_txt: bfloat16 [8, 64, 3072], P(('groups', 'shard'), 'seq'), parts along dimension 0, may hold values from -24 to 24
- out_w_img: bfloat16 [2048, 3072], P('seq', 'shard'), may hold values from -0.125 to 0.125
- out_w_txt: bfloat16 [2048, 3072], P('seq', 'shard'), may hold values from -0.125 to 0.125
Outputs:
- dqkv_img: bfloat16 [3, 8, 512, 2048], P(None, ('groups', 'shard'), 'seq'), parts along dimension 1
- dqkv_txt: bfloat16 [3, 8, 64, 2048], P(None, ('groups', 'shard'), 'seq'), parts along dimension 1
- dw_img: float32 [4096, 3072], P(('groups', 'seq'), 'shard'), parts along dimension 0
- dw_txt: float32 [4096, 3072], P(('groups', 'seq'), 'shard'), parts along dimension 0
The draws below stay inside these ranges and needn't reach their ends.
There are 2 independent parts, one for each index of `groups`. The reference program is written for one: setup_inputs(seed, part) draws one part's arguments, and reference() takes and returns one part's arrays. A program takes and returns all parts, laid end to end along the dimension named above; an argument that names none is the same for every part. Nothing has to cross between parts.
All inputs are finite; a program needn't handle non-finite values.
Results may differ from the reference program's by a relative error of at most 0.0085.
Values may be sent and summed in bfloat16 or wider, within the bound.
A program may use at most 64 MiB of HBM per device.

```python
import jax
import jax.numpy as jnp
from jax import lax

D = 3072
HEADS = 16
HEAD_DIM = 128
L_IMG = 512
L_TXT = 64
SEQ_LEN = 576
HD = 2048
IMAGES = 4


def draw_qkv_img(key, part):
    key = jax.random.fold_in(key, 17)
    shape = (3, IMAGES, L_IMG, HD)
    base = jax.random.normal(key, shape, jnp.float32) * 1.2
    return jnp.clip(base, -8.0, 8.0).astype(jnp.bfloat16)


def spiked(values, stream_key, source, target, blocks, factor):
    owner, partner = [(jnp.arange(values.shape[position]) // (values.shape[position] // blocks)).reshape([-1 if axis == position else 1 for axis in range(values.ndim)]) for position in (source, target)]
    chosen = jax.random.permutation(stream_key, blocks)[partner]
    strong = (owner == chosen) | (owner == (partner + blocks // 2) % blocks)
    return jnp.where(strong, factor * values, values)


def levels(rng, dims, pieces, low, top_value):
    level = 1.0
    for axis_at, blocks in pieces:
        draws = jax.random.uniform(jax.random.fold_in(jax.random.fold_in(rng, 6), axis_at), (blocks,), jnp.float32, low / len(pieces), top_value / len(pieces))
        level = level * jnp.repeat(jnp.exp(draws), dims[axis_at] // blocks).reshape((-1,) + (1,) * (len(dims) - 1 - axis_at))
    return level


def centred(rng, extent, width, most, shards=(), held_as=jnp.bfloat16):
    result = width * jax.random.normal(rng, extent, jnp.float32)
    if shards:
        result = result * levels(rng, extent, shards, -0.22, 0.18)
    return jnp.clip(result, -most, most).astype(held_as)


def noise_with(stream_key, shape, width, most, split, heavy, kind=jnp.bfloat16):
    array = width * jax.random.normal(stream_key, shape, jnp.float32)
    if split:
        array = array * levels(stream_key, shape, split, -0.22, 0.18)
    return jnp.clip(spiked(array, jax.random.fold_in(stream_key, 3), *heavy), -most, most).astype(kind)


def setup_inputs(seed: int = 0, part: int = 0) -> dict:
    key_of = jax.random.split(jax.random.key(seed), 7)
    part_keys = jax.random.split(jax.random.fold_in(key_of[6], part), 7)
    return {
        "qkv_img": draw_qkv_img(jax.random.fold_in(jax.random.fold_in(key_of[6], part), 71), part),
        "qkv_txt": centred(part_keys[1], (3, IMAGES, L_TXT, HD), 1.2, 8.0, ((1, 4), (2, 4))),
        "grad_img": noise_with(part_keys[2], (IMAGES, L_IMG, D), 4.0, 24.0, ((0, 4), (1, 4)), (0, 2, 4, 2.0)),
        "grad_txt": centred(part_keys[3], (IMAGES, L_TXT, D), 4.0, 24.0, ((0, 4), (1, 4))),
        "out_w_img": centred(key_of[4], (HD, D), HD ** -0.5, 0.125, ((0, 4), (1, 4))),
        "out_w_txt": centred(key_of[5], (HD, D), HD ** -0.5, 0.125, ((0, 4), (1, 4))),
    }


def head_backward(query, keys, values, dout):
    scale = HEAD_DIM ** -0.5
    scores = jnp.dot(query, keys.T, preferred_element_type=jnp.float32) * scale
    top = jnp.max(scores, axis=-1, keepdims=True)
    expo = jnp.exp(scores - top)
    probs = expo / jnp.sum(expo, axis=-1, keepdims=True)
    probs_low = probs.astype(jnp.bfloat16)
    output = jnp.dot(probs_low, values, preferred_element_type=jnp.float32)
    dprobs = jnp.dot(dout, values.T, preferred_element_type=jnp.float32)
    delta = jnp.sum(dout.astype(jnp.float32) * output, axis=-1, keepdims=True)
    dscore = (probs * (dprobs - delta)).astype(jnp.bfloat16)
    dquery = (jnp.dot(dscore, keys, preferred_element_type=jnp.float32) * scale).astype(jnp.bfloat16)
    dkeys = (jnp.dot(dscore.T, query, preferred_element_type=jnp.float32) * scale).astype(jnp.bfloat16)
    dvalues = jnp.dot(probs_low.T, dout, preferred_element_type=jnp.float32).astype(jnp.bfloat16)
    return output.astype(jnp.bfloat16), dquery, dkeys, dvalues


def arrange(block):
    return block.reshape(SEQ_LEN, HEADS, HEAD_DIM).transpose(1, 0, 2)


def restore(block):
    return block.transpose(1, 0, 2).reshape(SEQ_LEN, HD)


def reference(qkv_img, qkv_txt, grad_img, grad_txt, out_w_img, out_w_txt):
    def one_image(carry, items):
        image_part, text_part, cot_img, cot_txt = items
        joint = jnp.concatenate([text_part, image_part], axis=1)
        dout = jnp.concatenate([
            jnp.dot(cot_txt, out_w_txt.T, preferred_element_type=jnp.float32),
            jnp.dot(cot_img, out_w_img.T, preferred_element_type=jnp.float32)], axis=0).astype(jnp.bfloat16)
        results = lax.map(lambda xs: head_backward(*xs),
                          (arrange(joint[0]), arrange(joint[1]), arrange(joint[2]), arrange(dout)))
        output = restore(results[0])
        grads = jnp.stack([restore(results[1]), restore(results[2]), restore(results[3])])
        part_txt = jnp.dot(output[:L_TXT].T, cot_txt, preferred_element_type=jnp.float32)
        part_img = jnp.dot(output[L_TXT:].T, cot_img, preferred_element_type=jnp.float32)
        part_txt = lax.optimization_barrier(part_txt.astype(jnp.bfloat16)).astype(jnp.float32)
        part_img = lax.optimization_barrier(part_img.astype(jnp.bfloat16)).astype(jnp.float32)
        carry = (carry[0] + part_img, carry[1] + part_txt)
        return carry, (grads[:, L_TXT:], grads[:, :L_TXT])

    start = (jnp.zeros((HD, D), jnp.float32), jnp.zeros((HD, D), jnp.float32))
    items = (qkv_img.transpose(1, 0, 2, 3), qkv_txt.transpose(1, 0, 2, 3), grad_img, grad_txt)
    totals, stacked = lax.scan(one_image, start, items)
    dqkv_img = stacked[0].transpose(1, 0, 2, 3)
    dqkv_txt = stacked[1].transpose(1, 0, 2, 3)
    return dqkv_img, dqkv_txt, totals[0], totals[1]
```

```python
import jax
import jax.numpy as jnp
from jax import lax
from jax.sharding import PartitionSpec as P

HEAD_DIM = 128


def head_backward(query, keys, values, dout):
    scale = HEAD_DIM ** (-0.5)
    scores = jnp.dot(query, keys.T, preferred_element_type=jnp.float32) * scale
    top = jnp.max(scores, axis=-1, keepdims=True)
    expo = jnp.exp(scores - top)
    probs = expo / jnp.sum(expo, axis=-1, keepdims=True)
    probs_low = probs.astype(jnp.bfloat16)
    output = jnp.dot(probs_low, values, preferred_element_type=jnp.float32)
    dprobs = jnp.dot(dout, values.T, preferred_element_type=jnp.float32)
    delta = jnp.sum(dout.astype(jnp.float32) * output, axis=-1, keepdims=True)
    dscore = (probs * (dprobs - delta)).astype(jnp.bfloat16)
    dquery = (jnp.dot(dscore, keys, preferred_element_type=jnp.float32) * scale).astype(
        jnp.bfloat16
    )
    dkeys = (jnp.dot(dscore.T, query, preferred_element_type=jnp.float32) * scale).astype(
        jnp.bfloat16
    )
    dvalues = jnp.dot(probs_low.T, dout, preferred_element_type=jnp.float32).astype(jnp.bfloat16)
    return (output.astype(jnp.bfloat16), dquery, dkeys, dvalues)


def gather_weights(qkv_img, qkv_txt, grad_img, grad_txt, out_w_img, out_w_txt):
    heads_txt, heads_img = (
        lax.all_to_all(qkv_txt, "seq", split_axis=3, concat_axis=2, tiled=True),
        lax.all_to_all(qkv_img, "seq", split_axis=3, concat_axis=2, tiled=True),
    )
    weight_txt, weight_img = (
        lax.all_gather(out_w_txt, "shard", axis=1, tiled=True),
        lax.all_gather(out_w_img, "shard", axis=1, tiled=True),
    )
    full_txt, full_img = (
        lax.all_gather(grad_txt, "seq", axis=1, tiled=True),
        lax.all_gather(grad_img, "seq", axis=1, tiled=True),
    )
    cot_txt = full_txt[0]
    cot_img = full_img[0]
    text_len = cot_txt.shape[0]
    joint = jnp.concatenate([heads_txt[:, 0], heads_img[:, 0]], axis=1)
    total_len = joint.shape[1]
    local_width = joint.shape[2]
    head_count = local_width // HEAD_DIM
    dout = jnp.concatenate(
        [
            jnp.einsum("td,hd->th", cot_txt, weight_txt, preferred_element_type=jnp.float32),
            jnp.einsum("td,hd->th", cot_img, weight_img, preferred_element_type=jnp.float32),
        ],
        axis=0,
    ).astype(jnp.bfloat16)

    def arrange(block):
        return block.reshape(total_len, head_count, HEAD_DIM).transpose(1, 0, 2)

    def restore(block):
        return block.transpose(1, 0, 2).reshape(total_len, local_width)

    results = lax.map(
        lambda items: head_backward(*items),
        (arrange(joint[0]), arrange(joint[1]), arrange(joint[2]), arrange(dout)),
    )
    output = restore(results[0])
    grads = jnp.stack([restore(results[1]), restore(results[2]), restore(results[3])])
    back_txt = grads[:, None, :text_len]
    back_img = grads[:, None, text_len:]
    ret_txt, ret_img = (
        lax.all_to_all(back_txt, "seq", split_axis=2, concat_axis=3, tiled=True),
        lax.all_to_all(back_img, "seq", split_axis=2, concat_axis=3, tiled=True),
    )
    part_txt = jnp.dot(output[:text_len].T, cot_txt, preferred_element_type=jnp.float32)
    part_img = jnp.dot(output[text_len:].T, cot_img, preferred_element_type=jnp.float32)
    sum_txt, sum_img = (
        lax.psum_scatter(
            part_txt.astype(jnp.bfloat16), "shard", scatter_dimension=1, tiled=True
        ).astype(jnp.float32),
        lax.psum_scatter(
            part_img.astype(jnp.bfloat16), "shard", scatter_dimension=1, tiled=True
        ).astype(jnp.float32),
    )
    return (ret_img, ret_txt, sum_img, sum_txt)


def gather_tokens(qkv_img, qkv_txt, grad_img, grad_txt, out_w_img, out_w_txt):
    text = qkv_txt.shape[2]
    tokens = text + qkv_img.shape[2]
    seq = lax.axis_size("seq")
    shard = lax.axis_size("shard")
    grad = jnp.concatenate([grad_txt[0], grad_img[0]], axis=0)
    cols = grad.shape[1] // shard
    grad = lax.all_to_all(
        grad.reshape(tokens, shard, cols).transpose(1, 0, 2), "shard", 0, 0, tiled=True
    )
    joint = jnp.concatenate([qkv_txt[:, 0], qkv_img[:, 0]], axis=1)
    joint = lax.all_to_all(joint, "seq", split_axis=2, concat_axis=1, tiled=True)
    grad = lax.all_gather(grad, "seq", axis=1, tiled=False)
    cot_txt = grad[:, :, :text]
    cot_img = grad[:, :, text:]
    part = jnp.concatenate(
        [
            jnp.einsum("bstd,hd->bsth", cot_txt, out_w_txt, preferred_element_type=jnp.float32),
            jnp.einsum("bstd,hd->bsth", cot_img, out_w_img, preferred_element_type=jnp.float32),
        ],
        axis=2,
    ).astype(jnp.bfloat16)
    part = lax.all_to_all(part, "shard", 0, 0, tiled=True)
    width = joint.shape[2]
    heads = width // HEAD_DIM
    total = seq * tokens
    dout = jnp.sum(part.astype(jnp.float32), axis=0).astype(jnp.bfloat16).reshape(total, width)

    results = []
    for h in range(heads):
        c = slice(h * HEAD_DIM, (h + 1) * HEAD_DIM)
        results.append(head_backward(joint[0, :, c], joint[1, :, c], joint[2, :, c], dout[:, c]))
    output = jnp.concatenate([r[0] for r in results], axis=1)
    every = lax.all_gather(output, "shard", axis=0, tiled=False)
    grads = jnp.stack([jnp.concatenate([r[i] for r in results], axis=1) for i in (1, 2, 3)])
    back = lax.all_to_all(grads, "seq", split_axis=1, concat_axis=2, tiled=True)
    every = every.reshape(shard, seq, tokens, width)
    dw_txt = jnp.einsum(
        "bsth,bstd->hd", every[:, :, :text], cot_txt, preferred_element_type=jnp.float32
    )
    dw_img = jnp.einsum(
        "bsth,bstd->hd", every[:, :, text:], cot_img, preferred_element_type=jnp.float32
    )
    return back[:, None, text:], back[:, None, :text], dw_img, dw_txt


def local(qkv_img, qkv_txt, grad_img, grad_txt, out_w_img, out_w_txt):
    shard = lax.axis_size("shard")
    weight_rows = 2 * out_w_img.shape[1]
    token_rows = lax.axis_size("seq") * (qkv_img.shape[2] + qkv_txt.shape[2])
    args = (qkv_img, qkv_txt, grad_img, grad_txt, out_w_img, out_w_txt)
    if token_rows <= weight_rows:
        return gather_tokens(*args)
    return gather_weights(*args)


def solution(mesh):
    return jax.shard_map(
        local,
        mesh=mesh,
        in_specs=(
            P(None, ("groups", "shard"), "seq", None),
            P(None, ("groups", "shard"), "seq", None),
            P(("groups", "shard"), "seq", None),
            P(("groups", "shard"), "seq", None),
            P("seq", "shard"),
            P("seq", "shard"),
        ),
        out_specs=(
            P(None, ("groups", "shard"), "seq", None),
            P(None, ("groups", "shard"), "seq", None),
            P(("groups", "seq"), "shard"),
            P(("groups", "seq"), "shard"),
        ),
        check_vma=False,
    )
```

```python
import functools

import jax
import jax.numpy as jnp
from jax import lax
from jax.experimental import pallas as pl
from jax.experimental.pallas import tpu as pltpu
from jax.sharding import PartitionSpec as P

HEAD_DIM = 128


def head_backward(query, keys, values, dout):
    scale = HEAD_DIM ** (-0.5)
    scores = jnp.dot(query, keys.T, preferred_element_type=jnp.float32) * scale
    top = jnp.max(scores, axis=-1, keepdims=True)
    expo = jnp.exp(scores - top)
    probs = expo / jnp.sum(expo, axis=-1, keepdims=True)
    probs_low = probs.astype(jnp.bfloat16)
    output = jnp.dot(probs_low, values, preferred_element_type=jnp.float32)
    dprobs = jnp.dot(dout, values.T, preferred_element_type=jnp.float32)
    delta = jnp.sum(dout.astype(jnp.float32) * output, axis=-1, keepdims=True)
    dscore = (probs * (dprobs - delta)).astype(jnp.bfloat16)
    dquery = (jnp.dot(dscore, keys, preferred_element_type=jnp.float32) * scale).astype(
        jnp.bfloat16
    )
    dkeys = (jnp.dot(dscore.T, query, preferred_element_type=jnp.float32) * scale).astype(
        jnp.bfloat16
    )
    dvalues = jnp.dot(probs_low.T, dout, preferred_element_type=jnp.float32).astype(jnp.bfloat16)
    return (output.astype(jnp.bfloat16), dquery, dkeys, dvalues)


def gather_weights(qkv_img, qkv_txt, grad_img, grad_txt, out_w_img, out_w_txt):
    heads_txt, heads_img = (
        lax.all_to_all(qkv_txt, "seq", split_axis=3, concat_axis=2, tiled=True),
        lax.all_to_all(qkv_img, "seq", split_axis=3, concat_axis=2, tiled=True),
    )
    weight_txt, weight_img = (
        lax.all_gather(out_w_txt, "shard", axis=1, tiled=True),
        lax.all_gather(out_w_img, "shard", axis=1, tiled=True),
    )
    full_txt, full_img = (
        lax.all_gather(grad_txt, "seq", axis=1, tiled=True),
        lax.all_gather(grad_img, "seq", axis=1, tiled=True),
    )
    cot_txt = full_txt[0]
    cot_img = full_img[0]
    text_len = cot_txt.shape[0]
    joint = jnp.concatenate([heads_txt[:, 0], heads_img[:, 0]], axis=1)
    total_len = joint.shape[1]
    local_width = joint.shape[2]
    head_count = local_width // HEAD_DIM
    dout = jnp.concatenate(
        [
            jnp.einsum("td,hd->th", cot_txt, weight_txt, preferred_element_type=jnp.float32),
            jnp.einsum("td,hd->th", cot_img, weight_img, preferred_element_type=jnp.float32),
        ],
        axis=0,
    ).astype(jnp.bfloat16)

    def arrange(block):
        return block.reshape(total_len, head_count, HEAD_DIM).transpose(1, 0, 2)

    def restore(block):
        return block.transpose(1, 0, 2).reshape(total_len, local_width)

    results = lax.map(
        lambda items: head_backward(*items),
        (arrange(joint[0]), arrange(joint[1]), arrange(joint[2]), arrange(dout)),
    )
    output = restore(results[0])
    grads = jnp.stack([restore(results[1]), restore(results[2]), restore(results[3])])
    back_txt = grads[:, None, :text_len]
    back_img = grads[:, None, text_len:]
    ret_txt, ret_img = (
        lax.all_to_all(back_txt, "seq", split_axis=2, concat_axis=3, tiled=True),
        lax.all_to_all(back_img, "seq", split_axis=2, concat_axis=3, tiled=True),
    )
    part_txt = jnp.dot(output[:text_len].T, cot_txt, preferred_element_type=jnp.float32)
    part_img = jnp.dot(output[text_len:].T, cot_img, preferred_element_type=jnp.float32)
    sum_txt, sum_img = (
        lax.psum_scatter(
            part_txt.astype(jnp.bfloat16), "shard", scatter_dimension=1, tiled=True
        ).astype(jnp.float32),
        lax.psum_scatter(
            part_img.astype(jnp.bfloat16), "shard", scatter_dimension=1, tiled=True
        ).astype(jnp.float32),
    )
    return (ret_img, ret_txt, sum_img, sum_txt)


def gather_tokens(qkv_img, qkv_txt, grad_img, grad_txt, out_w_img, out_w_txt):
    text = qkv_txt.shape[2]
    tokens = text + qkv_img.shape[2]
    seq = lax.axis_size("seq")
    shard = lax.axis_size("shard")
    grad = jnp.concatenate([grad_txt[0], grad_img[0]], axis=0)
    cols = grad.shape[1] // shard
    grad = lax.all_to_all(
        grad.reshape(tokens, shard, cols).transpose(1, 0, 2), "shard", 0, 0, tiled=True
    )
    joint = jnp.concatenate([qkv_txt[:, 0], qkv_img[:, 0]], axis=1)
    joint = lax.all_to_all(joint, "seq", split_axis=2, concat_axis=1, tiled=True)
    grad = lax.all_gather(grad, "seq", axis=1, tiled=False)
    cot_txt = grad[:, :, :text]
    cot_img = grad[:, :, text:]
    part = jnp.concatenate(
        [
            jnp.einsum("bstd,hd->bsth", cot_txt, out_w_txt, preferred_element_type=jnp.float32),
            jnp.einsum("bstd,hd->bsth", cot_img, out_w_img, preferred_element_type=jnp.float32),
        ],
        axis=2,
    ).astype(jnp.bfloat16)
    part = lax.all_to_all(part, "shard", 0, 0, tiled=True)
    width = joint.shape[2]
    heads = width // HEAD_DIM
    total = seq * tokens
    dout = jnp.sum(part.astype(jnp.float32), axis=0).astype(jnp.bfloat16).reshape(total, width)

    results = []
    for h in range(heads):
        c = slice(h * HEAD_DIM, (h + 1) * HEAD_DIM)
        results.append(head_backward(joint[0, :, c], joint[1, :, c], joint[2, :, c], dout[:, c]))
    output = jnp.concatenate([r[0] for r in results], axis=1)
    every = lax.all_gather(output, "shard", axis=0, tiled=False)
    grads = jnp.stack([jnp.concatenate([r[i] for r in results], axis=1) for i in (1, 2, 3)])
    back = lax.all_to_all(grads, "seq", split_axis=1, concat_axis=2, tiled=True)
    every = every.reshape(shard, seq, tokens, width)
    dw_txt = jnp.einsum(
        "bsth,bstd->hd", every[:, :, :text], cot_txt, preferred_element_type=jnp.float32
    )
    dw_img = jnp.einsum(
        "bsth,bstd->hd", every[:, :, text:], cot_img, preferred_element_type=jnp.float32
    )
    return back[:, None, text:], back[:, None, :text], dw_img, dw_txt


NT = (((1,), (1,)), ((), ()))
TN = (((0,), (0,)), ((), ()))


def fused_kernel(
    S, Z, text, qkv_img, qkv_txt, grad_img, grad_txt, w_img, w_txt,
    out_img, out_txt, dw_img, dw_txt,
    gbuf, qbuf, heads, G, psend, part, own, probs_s, o_s, every, dout_s, dbuf, rbuf,
    local_sem, gz_s, gz_r, gx_s, gx_r, q_s, q_r, p_s, p_r, o_snd, o_r, d_s, d_r,
):
    T = gbuf.shape[0]
    C = w_img.shape[1]
    W = w_img.shape[0]
    H = W // HEAD_DIM
    s = lax.axis_index("seq")
    z = lax.axis_index("shard")
    core = s + 1 - 2 * lax.rem(s, 2)
    cross = lax.rem(s + 2, S)
    diag = lax.rem(core + 2, S)
    seqs = [core, cross, diag]
    imgs = [lax.rem(z + k, Z) for k in range(Z)]

    def rows(block):
        return pl.ds(pl.multiple_of(block * T, 16), T)

    def cols(block, width):
        return pl.ds(pl.multiple_of(block * width, 128), width)

    stage = [
        pltpu.make_async_copy(grad_txt.at[0], gbuf.at[pl.ds(0, text)], local_sem.at[0]),
        pltpu.make_async_copy(grad_img.at[0], gbuf.at[pl.ds(text, T - text)], local_sem.at[1]),
        pltpu.make_async_copy(qkv_txt.at[:, 0], qbuf.at[:, pl.ds(0, text)], local_sem.at[2]),
        pltpu.make_async_copy(
            qkv_img.at[:, 0], qbuf.at[:, pl.ds(text, T - text)], local_sem.at[3]
        ),
    ]
    for c in stage:
        c.start()
    barrier = pltpu.get_barrier_semaphore()
    for t in seqs:
        pl.semaphore_signal(
            barrier, inc=1, device_id={"seq": t}, device_id_type=pl.DeviceIdType.MESH
        )
    for t in imgs[1:]:
        pl.semaphore_signal(
            barrier, inc=1, device_id={"shard": t}, device_id_type=pl.DeviceIdType.MESH
        )
    pl.semaphore_wait(barrier, S + Z - 2)

    def remote(src, dst, send, recv, where):
        return pltpu.make_async_remote_copy(
            src_ref=src, dst_ref=dst, send_sem=send, recv_sem=recv,
            device_id=where, device_id_type=pl.DeviceIdType.MESH,
        )

    sends = []

    def start(*args):
        c = remote(*args)
        c.start()
        sends.append(c)

    def block(i, t):
        return G.at[i, rows(t)]

    def gx_start(i, t, kind, where):
        start(block(i, t), block(i, t), gx_s.at[i, kind], gx_r.at[i, kind], {"seq": where})

    def gx_wait(i, t, kind):
        remote(
            block(i, t), block(i, t), gx_s.at[i, kind], gx_r.at[i, kind], {"seq": core}
        ).wait_recv()

    stage[0].wait()
    stage[1].wait()
    for k in range(1, Z):
        i = imgs[k]
        start(gbuf.at[:, cols(i, C)], block(z, s), gz_s.at[k], gz_r.at[z], {"shard": i})
    mine = pltpu.make_async_copy(gbuf.at[:, cols(z, C)], block(z, s), local_sem.at[4])
    mine.start()
    mine.wait()
    gx_start(z, s, 0, cross)
    gx_start(z, s, 1, core)
    stage[2].wait()
    stage[3].wait()
    for n, t in enumerate((cross, diag, core)):
        start(qbuf.at[:, :, cols(t, W)], heads.at[:, rows(s)], q_s.at[n], q_r.at[s], {"seq": t})
    mine_q = pltpu.make_async_copy(qbuf.at[:, :, cols(s, W)], heads.at[:, rows(s)], local_sem.at[5])
    mine_q.start()

    def split(ref, i):
        image = jnp.concatenate([ref[i, t * T + text:(t + 1) * T, :] for t in range(S)], axis=0)
        words = jnp.concatenate([ref[i, t * T:t * T + text, :] for t in range(S)], axis=0)
        return image, words

    def partial(i, store):
        image, words = split(G, i)
        pi = lax.dot_general(image, w_img[...], NT, preferred_element_type=jnp.float32)
        pt = lax.dot_general(words, w_txt[...], NT, preferred_element_type=jnp.float32)
        n = T - text
        for t in range(S):
            store(t * T, text, pt[t * text:(t + 1) * text])
            store(t * T + text, n, pi[t * n:(t + 1) * n])

    def relay(k):
        gx_wait(imgs[k], cross, 0)
        gx_start(imgs[k], cross, 2, core)

    def produce(k):
        i = imgs[k]
        gx_wait(i, core, 1)
        gx_wait(i, diag, 2)

        def store(r, n, v):
            psend[k - 1, r:r + n, :] = v.astype(jnp.bfloat16)

        partial(i, store)
        start(psend.at[k - 1], part.at[z], p_s.at[k], p_r.at[z], {"shard": i})

    for k in range(1, Z):
        i = imgs[k]
        remote(block(i, s), block(i, s), gz_s.at[k], gz_r.at[i], {"shard": i}).wait_recv()
        gx_start(i, s, 0, cross)
        gx_start(i, s, 1, core)
        relay(k - 1)
        if k >= 3:
            produce(k - 2)
    relay(Z - 1)
    for k in range(max(1, Z - 2), Z):
        produce(k)
    gx_wait(z, core, 1)
    gx_wait(z, diag, 2)

    def store_own(r, n, v):
        own[r:r + n, :] = v

    partial(z, store_own)

    mine_q.wait()
    for t in seqs:
        remote(
            heads.at[:, rows(t)], heads.at[:, rows(t)], q_s.at[0], q_r.at[t], {"seq": t}
        ).wait_recv()
    scale = HEAD_DIM ** (-0.5)

    def forward(h, carry):
        c = cols(h, HEAD_DIM)
        scores = lax.dot_general(
            heads[0, :, c], heads[1, :, c], NT, preferred_element_type=jnp.float32
        ) * scale
        expo = jnp.exp(scores - jnp.max(scores, axis=-1, keepdims=True))
        probs = expo * (1.0 / jnp.sum(expo, axis=-1, keepdims=True))
        probs_s[h] = probs
        o = jnp.dot(probs.astype(jnp.bfloat16), heads[2, :, c], preferred_element_type=jnp.float32)
        o_s[:, c] = o
        every[z, :, c] = o.astype(jnp.bfloat16)
        return carry

    lax.fori_loop(0, H, forward, 0)
    for k in range(1, Z):
        start(every.at[z], every.at[z], o_snd.at[k], o_r.at[z], {"shard": imgs[k]})

    for k in range(1, Z):
        i = imgs[k]
        remote(part.at[i], part.at[i], p_s.at[k], p_r.at[i], {"shard": i}).wait_recv()
    total = own[...]
    for k in range(1, Z):
        total = total + part[imgs[k]].astype(jnp.float32)
    dout_s[...] = total.astype(jnp.bfloat16)

    def d_copy(h, n, t):
        return remote(
            dbuf.at[:, rows(t), cols(h, HEAD_DIM)],
            rbuf.at[:, :, cols(s * H + h, HEAD_DIM)],
            d_s.at[h, n], d_r.at[h, n], {"seq": t},
        )

    def backward(h, carry):
        c = cols(h, HEAD_DIM)
        dout = dout_s[:, c]
        probs = probs_s[h]
        dprobs = lax.dot_general(dout, heads[2, :, c], NT, preferred_element_type=jnp.float32)
        delta = jnp.sum(dout.astype(jnp.float32) * o_s[:, c], axis=-1, keepdims=True)
        ds = (probs * (dprobs - delta)).astype(jnp.bfloat16)
        dq = jnp.dot(ds, heads[1, :, c], preferred_element_type=jnp.float32) * scale
        dk = lax.dot_general(ds, heads[0, :, c], TN, preferred_element_type=jnp.float32) * scale
        dv = lax.dot_general(
            probs.astype(jnp.bfloat16), dout, TN, preferred_element_type=jnp.float32
        )
        dbuf[0, :, c] = dq.astype(jnp.bfloat16)
        dbuf[1, :, c] = dk.astype(jnp.bfloat16)
        dbuf[2, :, c] = dv.astype(jnp.bfloat16)
        for n, t in ((1, cross), (2, diag), (0, core)):
            d_copy(h, n, t).start()
        return carry

    lax.fori_loop(0, H, backward, 0)
    mine_d = pltpu.make_async_copy(dbuf.at[:, rows(s)], rbuf.at[:, :, cols(s, W)], local_sem.at[6])
    mine_d.start()

    for k in range(Z):
        i = imgs[k]
        if k:
            remote(every.at[i], every.at[i], o_snd.at[k], o_r.at[i], {"shard": i}).wait_recv()
        ob_i, ob_t = split(every, i)
        g_i, g_t = split(G, i)
        di = lax.dot_general(ob_i, g_i, TN, preferred_element_type=jnp.float32)
        dt = lax.dot_general(ob_t, g_t, TN, preferred_element_type=jnp.float32)
        if k:
            dw_img[...] += di
            dw_txt[...] += dt
        else:
            dw_img[...] = di
            dw_txt[...] = dt

    mine_d.wait()
    for h in range(H):
        for n, t in enumerate(seqs):
            d_copy(h, n, t).wait_send()
            remote(
                rbuf.at[:, :, cols(t * H + h, HEAD_DIM)],
                rbuf.at[:, :, cols(t * H + h, HEAD_DIM)],
                d_s.at[h, n], d_r.at[h, n], {"seq": t},
            ).wait_recv()
    last = [
        pltpu.make_async_copy(rbuf.at[:, pl.ds(0, text)], out_txt.at[:, 0], local_sem.at[0]),
        pltpu.make_async_copy(rbuf.at[:, pl.ds(text, T - text)], out_img.at[:, 0], local_sem.at[1]),
    ]
    for c in last:
        c.start()
    for c in sends:
        c.wait_send()
    for c in last:
        c.wait()


def fused(qkv_img, qkv_txt, grad_img, grad_txt, out_w_img, out_w_txt):
    S = lax.axis_size("seq")
    Z = lax.axis_size("shard")
    text = qkv_txt.shape[2]
    T = text + qkv_img.shape[2]
    HDW = qkv_img.shape[3]
    width = grad_img.shape[2]
    W, C = out_w_img.shape
    H = W // HEAD_DIM
    N = S * T
    bf, f4 = jnp.bfloat16, jnp.float32
    V, D = pltpu.VMEM, pltpu.SemaphoreType.DMA
    hbm = pl.BlockSpec(memory_space=pl.ANY)
    vm = pl.BlockSpec(memory_space=pltpu.VMEM)
    return pl.pallas_call(
        functools.partial(fused_kernel, S, Z, text),
        out_shape=(
            jax.ShapeDtypeStruct(qkv_img.shape, bf),
            jax.ShapeDtypeStruct(qkv_txt.shape, bf),
            jax.ShapeDtypeStruct((W, C), f4),
            jax.ShapeDtypeStruct((W, C), f4),
        ),
        in_specs=[hbm, hbm, hbm, hbm, vm, vm],
        out_specs=(hbm, hbm, vm, vm),
        scratch_shapes=[
            V((T, width), bf), V((3, T, HDW), bf), V((3, N, W), bf), V((Z, N, C), bf),
            V((Z - 1, N, W), bf), V((Z, N, W), bf), V((N, W), f4), V((H, N, N), f4),
            V((N, W), f4), V((Z, N, W), bf), V((N, W), bf), V((3, N, W), bf), V((3, T, HDW), bf),
            D((7,)), D((Z,)), D((Z,)), D((Z, 3)), D((Z, 3)), D((S,)), D((S,)),
            D((Z,)), D((Z,)), D((Z,)), D((Z,)), D((H, 3)), D((H, 3)),
        ],
        compiler_params=pltpu.CompilerParams(
            collective_id=0, has_side_effects=True, vmem_limit_bytes=52 * 1024 * 1024
        ),
    )(qkv_img, qkv_txt, grad_img, grad_txt, out_w_img, out_w_txt)


def local(qkv_img, qkv_txt, grad_img, grad_txt, out_w_img, out_w_txt):
    shard = lax.axis_size("shard")
    weight_rows = 2 * out_w_img.shape[1]
    token_rows = lax.axis_size("seq") * (qkv_img.shape[2] + qkv_txt.shape[2])
    args = (qkv_img, qkv_txt, grad_img, grad_txt, out_w_img, out_w_txt)
    if (
        token_rows <= weight_rows
        and lax.axis_size("seq") == 4
        and lax.axis_size("shard") == 4
        and out_w_img.shape[1] % 128 == 0
        and qkv_txt.shape[2] % 16 == 0
        and qkv_img.shape[2] % 16 == 0
    ):
        return fused(*args)
    if token_rows <= weight_rows:
        return gather_tokens(*args)
    return gather_weights(*args)


def solution(mesh):
    return jax.shard_map(
        local,
        mesh=mesh,
        in_specs=(
            P(None, ("groups", "shard"), "seq", None),
            P(None, ("groups", "shard"), "seq", None),
            P(("groups", "shard"), "seq", None),
            P(("groups", "shard"), "seq", None),
            P("seq", "shard"),
            P("seq", "shard"),
        ),
        out_specs=(
            P(None, ("groups", "shard"), "seq", None),
            P(None, ("groups", "shard"), "seq", None),
            P(("groups", "seq"), "shard"),
            P(("groups", "seq"), "shard"),
        ),
        check_vma=False,
    )
```

```python
import functools

import jax
import jax.numpy as jnp
from jax import lax
from jax.experimental import pallas as pl
from jax.experimental.pallas import tpu as pltpu
from jax.sharding import PartitionSpec as P

HEAD_DIM = 128


def head_backward(query, keys, values, dout):
    scale = HEAD_DIM ** (-0.5)
    scores = jnp.dot(query, keys.T, preferred_element_type=jnp.float32) * scale
    top = jnp.max(scores, axis=-1, keepdims=True)
    expo = jnp.exp(scores - top)
    probs = expo / jnp.sum(expo, axis=-1, keepdims=True)
    probs_low = probs.astype(jnp.bfloat16)
    output = jnp.dot(probs_low, values, preferred_element_type=jnp.float32)
    dprobs = jnp.dot(dout, values.T, preferred_element_type=jnp.float32)
    delta = jnp.sum(dout.astype(jnp.float32) * output, axis=-1, keepdims=True)
    dscore = (probs * (dprobs - delta)).astype(jnp.bfloat16)
    dquery = (jnp.dot(dscore, keys, preferred_element_type=jnp.float32) * scale).astype(
        jnp.bfloat16
    )
    dkeys = (jnp.dot(dscore.T, query, preferred_element_type=jnp.float32) * scale).astype(
        jnp.bfloat16
    )
    dvalues = jnp.dot(probs_low.T, dout, preferred_element_type=jnp.float32).astype(jnp.bfloat16)
    return (output.astype(jnp.bfloat16), dquery, dkeys, dvalues)


def gather_weights(qkv_img, qkv_txt, grad_img, grad_txt, out_w_img, out_w_txt):
    heads_txt, heads_img = (
        lax.all_to_all(qkv_txt, "seq", split_axis=3, concat_axis=2, tiled=True),
        lax.all_to_all(qkv_img, "seq", split_axis=3, concat_axis=2, tiled=True),
    )
    weight_txt, weight_img = (
        lax.all_gather(out_w_txt, "shard", axis=1, tiled=True),
        lax.all_gather(out_w_img, "shard", axis=1, tiled=True),
    )
    full_txt, full_img = (
        lax.all_gather(grad_txt, "seq", axis=1, tiled=True),
        lax.all_gather(grad_img, "seq", axis=1, tiled=True),
    )
    cot_txt = full_txt[0]
    cot_img = full_img[0]
    text_len = cot_txt.shape[0]
    joint = jnp.concatenate([heads_txt[:, 0], heads_img[:, 0]], axis=1)
    total_len = joint.shape[1]
    local_width = joint.shape[2]
    head_count = local_width // HEAD_DIM
    dout = jnp.concatenate(
        [
            jnp.einsum("td,hd->th", cot_txt, weight_txt, preferred_element_type=jnp.float32),
            jnp.einsum("td,hd->th", cot_img, weight_img, preferred_element_type=jnp.float32),
        ],
        axis=0,
    ).astype(jnp.bfloat16)

    def arrange(block):
        return block.reshape(total_len, head_count, HEAD_DIM).transpose(1, 0, 2)

    def restore(block):
        return block.transpose(1, 0, 2).reshape(total_len, local_width)

    results = lax.map(
        lambda items: head_backward(*items),
        (arrange(joint[0]), arrange(joint[1]), arrange(joint[2]), arrange(dout)),
    )
    output = restore(results[0])
    grads = jnp.stack([restore(results[1]), restore(results[2]), restore(results[3])])
    back_txt = grads[:, None, :text_len]
    back_img = grads[:, None, text_len:]
    ret_txt, ret_img = (
        lax.all_to_all(back_txt, "seq", split_axis=2, concat_axis=3, tiled=True),
        lax.all_to_all(back_img, "seq", split_axis=2, concat_axis=3, tiled=True),
    )
    part_txt = jnp.dot(output[:text_len].T, cot_txt, preferred_element_type=jnp.float32)
    part_img = jnp.dot(output[text_len:].T, cot_img, preferred_element_type=jnp.float32)
    sum_txt, sum_img = (
        lax.psum_scatter(
            part_txt.astype(jnp.bfloat16), "shard", scatter_dimension=1, tiled=True
        ).astype(jnp.float32),
        lax.psum_scatter(
            part_img.astype(jnp.bfloat16), "shard", scatter_dimension=1, tiled=True
        ).astype(jnp.float32),
    )
    return (ret_img, ret_txt, sum_img, sum_txt)


def gather_tokens(qkv_img, qkv_txt, grad_img, grad_txt, out_w_img, out_w_txt):
    text = qkv_txt.shape[2]
    tokens = text + qkv_img.shape[2]
    seq = lax.axis_size("seq")
    shard = lax.axis_size("shard")
    grad = jnp.concatenate([grad_txt[0], grad_img[0]], axis=0)
    cols = grad.shape[1] // shard
    grad = lax.all_to_all(
        grad.reshape(tokens, shard, cols).transpose(1, 0, 2), "shard", 0, 0, tiled=True
    )
    joint = jnp.concatenate([qkv_txt[:, 0], qkv_img[:, 0]], axis=1)
    joint = lax.all_to_all(joint, "seq", split_axis=2, concat_axis=1, tiled=True)
    grad = lax.all_gather(grad, "seq", axis=1, tiled=False)
    cot_txt = grad[:, :, :text]
    cot_img = grad[:, :, text:]
    part = jnp.concatenate(
        [
            jnp.einsum("bstd,hd->bsth", cot_txt, out_w_txt, preferred_element_type=jnp.float32),
            jnp.einsum("bstd,hd->bsth", cot_img, out_w_img, preferred_element_type=jnp.float32),
        ],
        axis=2,
    ).astype(jnp.bfloat16)
    part = lax.all_to_all(part, "shard", 0, 0, tiled=True)
    width = joint.shape[2]
    heads = width // HEAD_DIM
    total = seq * tokens
    dout = jnp.sum(part.astype(jnp.float32), axis=0).astype(jnp.bfloat16).reshape(total, width)

    results = []
    for h in range(heads):
        c = slice(h * HEAD_DIM, (h + 1) * HEAD_DIM)
        results.append(head_backward(joint[0, :, c], joint[1, :, c], joint[2, :, c], dout[:, c]))
    output = jnp.concatenate([r[0] for r in results], axis=1)
    every = lax.all_gather(output, "shard", axis=0, tiled=False)
    grads = jnp.stack([jnp.concatenate([r[i] for r in results], axis=1) for i in (1, 2, 3)])
    back = lax.all_to_all(grads, "seq", split_axis=1, concat_axis=2, tiled=True)
    every = every.reshape(shard, seq, tokens, width)
    dw_txt = jnp.einsum(
        "bsth,bstd->hd", every[:, :, :text], cot_txt, preferred_element_type=jnp.float32
    )
    dw_img = jnp.einsum(
        "bsth,bstd->hd", every[:, :, text:], cot_img, preferred_element_type=jnp.float32
    )
    return back[:, None, text:], back[:, None, :text], dw_img, dw_txt


NT = (((1,), (1,)), ((), ()))
TN = (((0,), (0,)), ((), ()))


def fused_kernel(
    S, Z, text, qkv_img, qkv_txt, grad_img, grad_txt, w_img, w_txt,
    out_img, out_txt, dw_img, dw_txt,
    gbuf, qbuf, heads, G, psend, part, own, probs_s, o_s, every, dbuf, rbuf,
    local_sem, gz_s, gz_r, gx_s, gx_r, q_s, q_r, p_s, p_r, o_snd, o_r, d_s, d_r,
):
    T = gbuf.shape[0]
    C = w_img.shape[1]
    W = w_img.shape[0]
    H = W // HEAD_DIM
    s = lax.axis_index("seq")
    z = lax.axis_index("shard")
    core = s + 1 - 2 * lax.rem(s, 2)
    cross = lax.rem(s + 2, S)
    diag = lax.rem(core + 2, S)
    seqs = [core, cross, diag]
    imgs = [lax.rem(z + k, Z) for k in range(Z)]

    def rows(block):
        return pl.ds(pl.multiple_of(block * T, 16), T)

    def cols(block, width):
        return pl.ds(pl.multiple_of(block * width, 128), width)

    stage = [
        pltpu.make_async_copy(grad_txt.at[0], gbuf.at[pl.ds(0, text)], local_sem.at[0]),
        pltpu.make_async_copy(grad_img.at[0], gbuf.at[pl.ds(text, T - text)], local_sem.at[1]),
        pltpu.make_async_copy(qkv_txt.at[:, 0], qbuf.at[:, pl.ds(0, text)], local_sem.at[2]),
        pltpu.make_async_copy(
            qkv_img.at[:, 0], qbuf.at[:, pl.ds(text, T - text)], local_sem.at[3]
        ),
    ]
    for c in stage:
        c.start()
    barrier = pltpu.get_barrier_semaphore()
    for t in seqs:
        pl.semaphore_signal(
            barrier, inc=1, device_id={"seq": t}, device_id_type=pl.DeviceIdType.MESH
        )
    for t in imgs[1:]:
        pl.semaphore_signal(
            barrier, inc=1, device_id={"shard": t}, device_id_type=pl.DeviceIdType.MESH
        )
    pl.semaphore_wait(barrier, S + Z - 2)

    def remote(src, dst, send, recv, where):
        return pltpu.make_async_remote_copy(
            src_ref=src, dst_ref=dst, send_sem=send, recv_sem=recv,
            device_id=where, device_id_type=pl.DeviceIdType.MESH,
        )

    sends = []

    def start(*args):
        c = remote(*args)
        c.start()
        sends.append(c)

    def block(i, t):
        return G.at[i, rows(t)]

    def gx_start(i, t, kind, where):
        start(block(i, t), block(i, t), gx_s.at[i, kind], gx_r.at[i, kind], {"seq": where})

    def gx_wait(i, t, kind):
        remote(
            block(i, t), block(i, t), gx_s.at[i, kind], gx_r.at[i, kind], {"seq": core}
        ).wait_recv()

    stage[0].wait()
    stage[1].wait()
    for k in range(1, Z):
        i = imgs[k]
        start(gbuf.at[:, cols(i, C)], block(z, s), gz_s.at[k], gz_r.at[z], {"shard": i})
    mine = pltpu.make_async_copy(gbuf.at[:, cols(z, C)], block(z, s), local_sem.at[4])
    mine.start()
    mine.wait()
    gx_start(z, s, 0, cross)
    gx_start(z, s, 1, core)
    stage[2].wait()
    stage[3].wait()
    for n, t in enumerate((cross, diag, core)):
        start(qbuf.at[:, :, cols(t, W)], heads.at[:, rows(s)], q_s.at[n], q_r.at[s], {"seq": t})
    mine_q = pltpu.make_async_copy(qbuf.at[:, :, cols(s, W)], heads.at[:, rows(s)], local_sem.at[5])
    mine_q.start()

    def split(ref, i):
        image = jnp.concatenate([ref[i, t * T + text:(t + 1) * T, :] for t in range(S)], axis=0)
        words = jnp.concatenate([ref[i, t * T:t * T + text, :] for t in range(S)], axis=0)
        return image, words

    def partial(i, store):
        image, words = split(G, i)
        pi = lax.dot_general(image, w_img[...], NT, preferred_element_type=jnp.float32)
        pt = lax.dot_general(words, w_txt[...], NT, preferred_element_type=jnp.float32)
        n = T - text
        for t in range(S):
            store(t * T, text, pt[t * text:(t + 1) * text])
            store(t * T + text, n, pi[t * n:(t + 1) * n])

    def relay(k):
        gx_wait(imgs[k], cross, 0)
        gx_start(imgs[k], cross, 2, core)

    def produce(k):
        i = imgs[k]
        gx_wait(i, core, 1)
        gx_wait(i, diag, 2)

        def store(r, n, v):
            psend[k - 1, r:r + n, :] = v.astype(jnp.bfloat16)

        partial(i, store)

    scale = HEAD_DIM ** (-0.5)

    def forward(h, carry):
        c = cols(h, HEAD_DIM)
        scores = lax.dot_general(
            heads[0, :, c], heads[1, :, c], NT, preferred_element_type=jnp.float32
        ) * scale
        expo = jnp.exp(scores - jnp.max(scores, axis=-1, keepdims=True))
        probs = expo * (1.0 / jnp.sum(expo, axis=-1, keepdims=True))
        probs_s[h] = probs
        o = jnp.dot(probs.astype(jnp.bfloat16), heads[2, :, c], preferred_element_type=jnp.float32)
        o_s[:, c] = o
        every[z, :, c] = o.astype(jnp.bfloat16)
        return carry

    for k in range(1, Z):
        i = imgs[k]
        remote(block(i, s), block(i, s), gz_s.at[k], gz_r.at[i], {"shard": i}).wait_recv()
        gx_start(i, s, 0, cross)
        gx_start(i, s, 1, core)
    mine_q.wait()
    for t in seqs:
        remote(
            heads.at[:, rows(t)], heads.at[:, rows(t)], q_s.at[0], q_r.at[t], {"seq": t}
        ).wait_recv()

    def o_copy(j, way, to):
        return remote(every.at[j], every.at[j], o_snd.at[j, way], o_r.at[j], {"shard": to})

    def hop(distance, act):
        left, right = z - distance, z + distance

        @pl.when((left >= 0) & (z < Z - 1))
        def _():
            act(o_copy(left, 0, z + 1))

        @pl.when((right < Z) & (z > 0))
        def _():
            act(o_copy(right, 1, z - 1))

    def arrive(distance):
        for j, ok in ((z - distance, z >= distance), (z + distance, z + distance < Z)):

            @pl.when(ok)
            def _():
                remote(every.at[j], every.at[j], o_snd.at[j, 0], o_r.at[j], {"shard": imgs[1]}).wait_recv()

    per = -(-H // Z)
    for k in range(Z):
        lax.fori_loop(min(H, k * per), min(H, (k + 1) * per), forward, 0)
        if k < Z - 1:
            relay(k)
    hop(0, lambda c: c.start())
    relay(Z - 1)
    for k in range(1, Z):
        produce(k)
    if Z > 2:
        arrive(1)
        hop(1, lambda c: c.start())
    for h in range(H):
        c = pl.ds(h * HEAD_DIM, HEAD_DIM)
        for k in range(Z - 1, 0, -1):
            start(
                psend.at[k - 1, :, c], part.at[z, :, c],
                p_s.at[k, h], p_r.at[z, h], {"shard": imgs[k]},
            )
    gx_wait(z, core, 1)
    gx_wait(z, diag, 2)

    def store_own(r, n, v):
        own[r:r + n, :] = v

    partial(z, store_own)

    def weight_grad(i):
        ob_i, ob_t = split(every, i)
        g_i, g_t = split(G, i)
        di = lax.dot_general(ob_i, g_i, TN, preferred_element_type=jnp.float32)
        dt = lax.dot_general(ob_t, g_t, TN, preferred_element_type=jnp.float32)
        return di, dt

    dw_img[...], dw_txt[...] = weight_grad(z)

    def d_copy(h, n, t):
        return remote(
            dbuf.at[:, rows(t), cols(h, HEAD_DIM)],
            rbuf.at[:, :, cols(s * H + h, HEAD_DIM)],
            d_s.at[h, n], d_r.at[h, n], {"seq": t},
        )

    def backward(h, carry):
        c = cols(h, HEAD_DIM)
        total = own[:, c]
        for k in range(1, Z):
            i = imgs[k]
            remote(
                part.at[i, :, c], part.at[i, :, c], p_s.at[k, h], p_r.at[i, h], {"shard": i}
            ).wait_recv()
            total = total + part[i, :, c].astype(jnp.float32)
        dout = total.astype(jnp.bfloat16)
        probs = probs_s[h]
        dprobs = lax.dot_general(dout, heads[2, :, c], NT, preferred_element_type=jnp.float32)
        delta = jnp.sum(dout.astype(jnp.float32) * o_s[:, c], axis=-1, keepdims=True)
        ds = (probs * (dprobs - delta)).astype(jnp.bfloat16)
        dq = jnp.dot(ds, heads[1, :, c], preferred_element_type=jnp.float32) * scale
        dk = lax.dot_general(ds, heads[0, :, c], TN, preferred_element_type=jnp.float32) * scale
        dv = lax.dot_general(
            probs.astype(jnp.bfloat16), dout, TN, preferred_element_type=jnp.float32
        )
        dbuf[0, :, c] = dq.astype(jnp.bfloat16)
        dbuf[1, :, c] = dk.astype(jnp.bfloat16)
        dbuf[2, :, c] = dv.astype(jnp.bfloat16)
        for n, t in ((1, cross), (2, diag), (0, core)):
            d_copy(h, n, t).start()
        return carry

    half = (H + 1) // 2
    lax.fori_loop(0, half, backward, 0)
    for distance in range(2, Z - 1):
        arrive(distance)
        hop(distance, lambda c: c.start())
    lax.fori_loop(half, H, backward, 0)
    mine_d = pltpu.make_async_copy(dbuf.at[:, rows(s)], rbuf.at[:, :, cols(s, W)], local_sem.at[6])
    mine_d.start()
    for distance in range(max(1, Z - 1), Z):
        arrive(distance)

    def add_image(k, carry):
        di, dt = weight_grad(lax.rem(z + k, Z))
        dw_img[...] += di
        dw_txt[...] += dt
        return carry

    lax.fori_loop(1, Z, add_image, 0)

    mine_d.wait()
    for h in range(H):
        for n, t in enumerate(seqs):
            d_copy(h, n, t).wait_send()
            remote(
                rbuf.at[:, :, cols(t * H + h, HEAD_DIM)],
                rbuf.at[:, :, cols(t * H + h, HEAD_DIM)],
                d_s.at[h, n], d_r.at[h, n], {"seq": t},
            ).wait_recv()
    last = [
        pltpu.make_async_copy(rbuf.at[:, pl.ds(0, text)], out_txt.at[:, 0], local_sem.at[0]),
        pltpu.make_async_copy(rbuf.at[:, pl.ds(text, T - text)], out_img.at[:, 0], local_sem.at[1]),
    ]
    for c in last:
        c.start()
    for c in sends:
        c.wait_send()
    for distance in range(Z - 1):
        hop(distance, lambda c: c.wait_send())
    for c in last:
        c.wait()


def fused(qkv_img, qkv_txt, grad_img, grad_txt, out_w_img, out_w_txt):
    S = lax.axis_size("seq")
    Z = lax.axis_size("shard")
    text = qkv_txt.shape[2]
    T = text + qkv_img.shape[2]
    HDW = qkv_img.shape[3]
    width = grad_img.shape[2]
    W, C = out_w_img.shape
    H = W // HEAD_DIM
    N = S * T
    bf, f4 = jnp.bfloat16, jnp.float32
    V, D = pltpu.VMEM, pltpu.SemaphoreType.DMA
    hbm = pl.BlockSpec(memory_space=pl.ANY)
    vm = pl.BlockSpec(memory_space=pltpu.VMEM)
    return pl.pallas_call(
        functools.partial(fused_kernel, S, Z, text),
        out_shape=(
            jax.ShapeDtypeStruct(qkv_img.shape, bf),
            jax.ShapeDtypeStruct(qkv_txt.shape, bf),
            jax.ShapeDtypeStruct((W, C), f4),
            jax.ShapeDtypeStruct((W, C), f4),
        ),
        in_specs=[hbm, hbm, hbm, hbm, vm, vm],
        out_specs=(hbm, hbm, vm, vm),
        scratch_shapes=[
            V((T, width), bf), V((3, T, HDW), bf), V((3, N, W), bf), V((Z, N, C), bf),
            V((Z - 1, N, W), bf), V((Z, N, W), bf), V((N, W), f4), V((H, N, N), f4),
            V((N, W), f4), V((Z, N, W), bf), V((3, N, W), bf), V((3, T, HDW), bf),
            D((7,)), D((Z,)), D((Z,)), D((Z, 3)), D((Z, 3)), D((S,)), D((S,)),
            D((Z, H)), D((Z, H)), D((Z, 2)), D((Z,)), D((H, 3)), D((H, 3)),
        ],
        compiler_params=pltpu.CompilerParams(
            collective_id=0, has_side_effects=True, vmem_limit_bytes=52 * 1024 * 1024
        ),
    )(qkv_img, qkv_txt, grad_img, grad_txt, out_w_img, out_w_txt)


def local(qkv_img, qkv_txt, grad_img, grad_txt, out_w_img, out_w_txt):
    shard = lax.axis_size("shard")
    weight_rows = 2 * out_w_img.shape[1]
    token_rows = lax.axis_size("seq") * (qkv_img.shape[2] + qkv_txt.shape[2])
    args = (qkv_img, qkv_txt, grad_img, grad_txt, out_w_img, out_w_txt)
    if (
        token_rows <= weight_rows
        and lax.axis_size("seq") == 4
        and lax.axis_size("shard") == 4
        and out_w_img.shape[1] % 128 == 0
        and qkv_txt.shape[2] % 16 == 0
        and qkv_img.shape[2] % 16 == 0
    ):
        return fused(*args)
    if token_rows <= weight_rows:
        return gather_tokens(*args)
    return gather_weights(*args)


def solution(mesh):
    return jax.shard_map(
        local,
        mesh=mesh,
        in_specs=(
            P(None, ("groups", "shard"), "seq", None),
            P(None, ("groups", "shard"), "seq", None),
            P(("groups", "shard"), "seq", None),
            P(("groups", "shard"), "seq", None),
            P("seq", "shard"),
            P("seq", "shard"),
        ),
        out_specs=(
            P(None, ("groups", "shard"), "seq", None),
            P(None, ("groups", "shard"), "seq", None),
            P(("groups", "seq"), "shard"),
            P(("groups", "seq"), "shard"),
        ),
        check_vma=False,
    )
```

```python
import functools

import jax
import jax.numpy as jnp
from jax import lax
from jax.experimental import pallas as pl
from jax.experimental.pallas import tpu as pltpu
from jax.sharding import PartitionSpec as P

HEAD_DIM = 128


def head_backward(query, keys, values, dout):
    scale = HEAD_DIM ** (-0.5)
    scores = jnp.dot(query, keys.T, preferred_element_type=jnp.float32) * scale
    top = jnp.max(scores, axis=-1, keepdims=True)
    expo = jnp.exp(scores - top)
    probs = expo / jnp.sum(expo, axis=-1, keepdims=True)
    probs_low = probs.astype(jnp.bfloat16)
    output = jnp.dot(probs_low, values, preferred_element_type=jnp.float32)
    dprobs = jnp.dot(dout, values.T, preferred_element_type=jnp.float32)
    delta = jnp.sum(dout.astype(jnp.float32) * output, axis=-1, keepdims=True)
    dscore = (probs * (dprobs - delta)).astype(jnp.bfloat16)
    dquery = (jnp.dot(dscore, keys, preferred_element_type=jnp.float32) * scale).astype(
        jnp.bfloat16
    )
    dkeys = (jnp.dot(dscore.T, query, preferred_element_type=jnp.float32) * scale).astype(
        jnp.bfloat16
    )
    dvalues = jnp.dot(probs_low.T, dout, preferred_element_type=jnp.float32).astype(jnp.bfloat16)
    return (output.astype(jnp.bfloat16), dquery, dkeys, dvalues)


def gather_weights(qkv_img, qkv_txt, grad_img, grad_txt, out_w_img, out_w_txt):
    heads_txt, heads_img = (
        lax.all_to_all(qkv_txt, "seq", split_axis=3, concat_axis=2, tiled=True),
        lax.all_to_all(qkv_img, "seq", split_axis=3, concat_axis=2, tiled=True),
    )
    weight_txt, weight_img = (
        lax.all_gather(out_w_txt, "shard", axis=1, tiled=True),
        lax.all_gather(out_w_img, "shard", axis=1, tiled=True),
    )
    full_txt, full_img = (
        lax.all_gather(grad_txt, "seq", axis=1, tiled=True),
        lax.all_gather(grad_img, "seq", axis=1, tiled=True),
    )
    cot_txt = full_txt[0]
    cot_img = full_img[0]
    text_len = cot_txt.shape[0]
    joint = jnp.concatenate([heads_txt[:, 0], heads_img[:, 0]], axis=1)
    total_len = joint.shape[1]
    local_width = joint.shape[2]
    head_count = local_width // HEAD_DIM
    dout = jnp.concatenate(
        [
            jnp.einsum("td,hd->th", cot_txt, weight_txt, preferred_element_type=jnp.float32),
            jnp.einsum("td,hd->th", cot_img, weight_img, preferred_element_type=jnp.float32),
        ],
        axis=0,
    ).astype(jnp.bfloat16)

    def arrange(block):
        return block.reshape(total_len, head_count, HEAD_DIM).transpose(1, 0, 2)

    def restore(block):
        return block.transpose(1, 0, 2).reshape(total_len, local_width)

    results = lax.map(
        lambda items: head_backward(*items),
        (arrange(joint[0]), arrange(joint[1]), arrange(joint[2]), arrange(dout)),
    )
    output = restore(results[0])
    grads = jnp.stack([restore(results[1]), restore(results[2]), restore(results[3])])
    back_txt = grads[:, None, :text_len]
    back_img = grads[:, None, text_len:]
    ret_txt, ret_img = (
        lax.all_to_all(back_txt, "seq", split_axis=2, concat_axis=3, tiled=True),
        lax.all_to_all(back_img, "seq", split_axis=2, concat_axis=3, tiled=True),
    )
    part_txt = jnp.dot(output[:text_len].T, cot_txt, preferred_element_type=jnp.float32)
    part_img = jnp.dot(output[text_len:].T, cot_img, preferred_element_type=jnp.float32)
    sum_txt, sum_img = (
        lax.psum_scatter(
            part_txt.astype(jnp.bfloat16), "shard", scatter_dimension=1, tiled=True
        ).astype(jnp.float32),
        lax.psum_scatter(
            part_img.astype(jnp.bfloat16), "shard", scatter_dimension=1, tiled=True
        ).astype(jnp.float32),
    )
    return (ret_img, ret_txt, sum_img, sum_txt)


def gather_tokens(qkv_img, qkv_txt, grad_img, grad_txt, out_w_img, out_w_txt):
    text = qkv_txt.shape[2]
    tokens = text + qkv_img.shape[2]
    seq = lax.axis_size("seq")
    shard = lax.axis_size("shard")
    grad = jnp.concatenate([grad_txt[0], grad_img[0]], axis=0)
    cols = grad.shape[1] // shard
    grad = lax.all_to_all(
        grad.reshape(tokens, shard, cols).transpose(1, 0, 2), "shard", 0, 0, tiled=True
    )
    joint = jnp.concatenate([qkv_txt[:, 0], qkv_img[:, 0]], axis=1)
    joint = lax.all_to_all(joint, "seq", split_axis=2, concat_axis=1, tiled=True)
    grad = lax.all_gather(grad, "seq", axis=1, tiled=False)
    cot_txt = grad[:, :, :text]
    cot_img = grad[:, :, text:]
    part = jnp.concatenate(
        [
            jnp.einsum("bstd,hd->bsth", cot_txt, out_w_txt, preferred_element_type=jnp.float32),
            jnp.einsum("bstd,hd->bsth", cot_img, out_w_img, preferred_element_type=jnp.float32),
        ],
        axis=2,
    ).astype(jnp.bfloat16)
    part = lax.all_to_all(part, "shard", 0, 0, tiled=True)
    width = joint.shape[2]
    heads = width // HEAD_DIM
    total = seq * tokens
    dout = jnp.sum(part.astype(jnp.float32), axis=0).astype(jnp.bfloat16).reshape(total, width)

    results = []
    for h in range(heads):
        c = slice(h * HEAD_DIM, (h + 1) * HEAD_DIM)
        results.append(head_backward(joint[0, :, c], joint[1, :, c], joint[2, :, c], dout[:, c]))
    output = jnp.concatenate([r[0] for r in results], axis=1)
    every = lax.all_gather(output, "shard", axis=0, tiled=False)
    grads = jnp.stack([jnp.concatenate([r[i] for r in results], axis=1) for i in (1, 2, 3)])
    back = lax.all_to_all(grads, "seq", split_axis=1, concat_axis=2, tiled=True)
    every = every.reshape(shard, seq, tokens, width)
    dw_txt = jnp.einsum(
        "bsth,bstd->hd", every[:, :, :text], cot_txt, preferred_element_type=jnp.float32
    )
    dw_img = jnp.einsum(
        "bsth,bstd->hd", every[:, :, text:], cot_img, preferred_element_type=jnp.float32
    )
    return back[:, None, text:], back[:, None, :text], dw_img, dw_txt


NT = (((1,), (1,)), ((), ()))
TN = (((0,), (0,)), ((), ()))


def fused_kernel(
    S, Z, text, qkv_img, qkv_txt, grad_img, grad_txt, w_img, w_txt,
    out_img, out_txt, dw_img, dw_txt,
    gbuf, qbuf, heads, G, psend, part, own, probs_s, o_s, every, dbuf, rbuf,
    local_sem, gz_s, gz_r, gx_s, gx_r, q_s, q_r, p_s, p_r, o_snd, o_r, d_s, d_r,
):
    T = gbuf.shape[0]
    C = w_img.shape[1]
    W = w_img.shape[0]
    H = W // HEAD_DIM
    s = lax.axis_index("seq")
    z = lax.axis_index("shard")
    core = s + 1 - 2 * lax.rem(s, 2)
    cross = lax.rem(s + 2, S)
    diag = lax.rem(core + 2, S)
    seqs = [core, cross, diag]
    imgs = [lax.rem(z + k, Z) for k in range(Z)]

    def rows(block):
        return pl.ds(pl.multiple_of(block * T, 16), T)

    def cols(block, width):
        if isinstance(block, int):
            return pl.ds(block * width, width)
        return pl.ds(pl.multiple_of(block * width, 128), width)

    stage = [
        pltpu.make_async_copy(grad_txt.at[0], gbuf.at[pl.ds(0, text)], local_sem.at[0]),
        pltpu.make_async_copy(grad_img.at[0], gbuf.at[pl.ds(text, T - text)], local_sem.at[1]),
        pltpu.make_async_copy(qkv_txt.at[:, 0], qbuf.at[:, pl.ds(0, text)], local_sem.at[2]),
        pltpu.make_async_copy(
            qkv_img.at[:, 0], qbuf.at[:, pl.ds(text, T - text)], local_sem.at[3]
        ),
    ]
    for c in stage:
        c.start()
    barrier = pltpu.get_barrier_semaphore()
    for t in seqs:
        pl.semaphore_signal(
            barrier, inc=1, device_id={"seq": t}, device_id_type=pl.DeviceIdType.MESH
        )
    for t in imgs[1:]:
        pl.semaphore_signal(
            barrier, inc=1, device_id={"shard": t}, device_id_type=pl.DeviceIdType.MESH
        )
    pl.semaphore_wait(barrier, S + Z - 2)

    def remote(src, dst, send, recv, where):
        return pltpu.make_async_remote_copy(
            src_ref=src, dst_ref=dst, send_sem=send, recv_sem=recv,
            device_id=where, device_id_type=pl.DeviceIdType.MESH,
        )

    sends = []

    def start(*args):
        c = remote(*args)
        c.start()
        sends.append(c)

    def block(i, t):
        return G.at[i, rows(t)]

    def gx_start(i, t, kind, where):
        start(block(i, t), block(i, t), gx_s.at[i, kind], gx_r.at[i, kind], {"seq": where})

    def gx_wait(i, t, kind):
        remote(
            block(i, t), block(i, t), gx_s.at[i, kind], gx_r.at[i, kind], {"seq": core}
        ).wait_recv()

    stage[0].wait()
    stage[1].wait()
    for k in range(1, Z):
        i = imgs[k]
        start(gbuf.at[:, cols(i, C)], block(z, s), gz_s.at[k], gz_r.at[z], {"shard": i})
    mine = pltpu.make_async_copy(gbuf.at[:, cols(z, C)], block(z, s), local_sem.at[4])
    mine.start()
    mine.wait()
    gx_start(z, s, 0, cross)
    gx_start(z, s, 1, core)
    stage[2].wait()
    stage[3].wait()
    for n, t in enumerate((cross, diag, core)):
        start(qbuf.at[:, :, cols(t, W)], heads.at[:, rows(s)], q_s.at[n], q_r.at[s], {"seq": t})
    mine_q = pltpu.make_async_copy(qbuf.at[:, :, cols(s, W)], heads.at[:, rows(s)], local_sem.at[5])
    mine_q.start()

    def split(ref, i):
        image = jnp.concatenate([ref[i, t * T + text:(t + 1) * T, :] for t in range(S)], axis=0)
        words = jnp.concatenate([ref[i, t * T:t * T + text, :] for t in range(S)], axis=0)
        return image, words

    def partial(i, store):
        image, words = split(G, i)
        pi = lax.dot_general(image, w_img[...], NT, preferred_element_type=jnp.float32)
        pt = lax.dot_general(words, w_txt[...], NT, preferred_element_type=jnp.float32)
        n = T - text
        for t in range(S):
            store(t * T, text, pt[t * text:(t + 1) * text])
            store(t * T + text, n, pi[t * n:(t + 1) * n])

    def relay(k):
        gx_wait(imgs[k], cross, 0)
        gx_start(imgs[k], cross, 2, core)

    def produce(k):
        i = imgs[k]
        gx_wait(i, core, 1)
        gx_wait(i, diag, 2)

        def store(r, n, v):
            psend[k - 1, r:r + n, :] = v.astype(jnp.bfloat16)

        partial(i, store)

    scale = HEAD_DIM ** (-0.5)

    def forward(h, carry):
        c = cols(h, HEAD_DIM)
        scores = lax.dot_general(
            heads[0, :, c], heads[1, :, c], NT, preferred_element_type=jnp.float32
        ) * scale
        expo = jnp.exp(scores - jnp.max(scores, axis=-1, keepdims=True))
        probs = expo * (1.0 / jnp.sum(expo, axis=-1, keepdims=True))
        probs_s[h] = probs
        o = jnp.dot(probs.astype(jnp.bfloat16), heads[2, :, c], preferred_element_type=jnp.float32)
        o_s[:, c] = o
        every[z, :, c] = o.astype(jnp.bfloat16)
        return carry

    for k in range(1, Z):
        i = imgs[k]
        remote(block(i, s), block(i, s), gz_s.at[k], gz_r.at[i], {"shard": i}).wait_recv()
        gx_start(i, s, 0, cross)
        gx_start(i, s, 1, core)
    mine_q.wait()
    for t in seqs:
        remote(
            heads.at[:, rows(t)], heads.at[:, rows(t)], q_s.at[0], q_r.at[t], {"seq": t}
        ).wait_recv()

    def o_copy(j, way, to):
        return remote(every.at[j], every.at[j], o_snd.at[j, way], o_r.at[j], {"shard": to})

    def hop(distance, act):
        left, right = z - distance, z + distance

        @pl.when((left >= 0) & (z < Z - 1))
        def _():
            act(o_copy(left, 0, z + 1))

        @pl.when((right < Z) & (z > 0))
        def _():
            act(o_copy(right, 1, z - 1))

    def arrive(distance):
        for j, ok in ((z - distance, z >= distance), (z + distance, z + distance < Z)):

            @pl.when(ok)
            def _():
                remote(every.at[j], every.at[j], o_snd.at[j, 0], o_r.at[j], {"shard": imgs[1]}).wait_recv()

    per = -(-H // Z)
    for k in range(Z):
        lax.fori_loop(min(H, k * per), min(H, (k + 1) * per), forward, 0)
        if k < Z - 1:
            relay(k)
    hop(0, lambda c: c.start())
    relay(Z - 1)
    for k in range(1, Z):
        produce(k)

    def chain(h, here, d, ahead, first):
        c = cols(h, HEAD_DIM)
        mine_k = (d - here) % Z - 1
        if not first:
            remote(
                part.at[d, :, c], part.at[d, :, c], p_s.at[d, h], p_r.at[d, h], {"shard": ahead}
            ).wait_recv()
            psend[mine_k, :, c] = (
                psend[mine_k, :, c].astype(jnp.float32) + part[d, :, c].astype(jnp.float32)
            ).astype(jnp.bfloat16)
        slot = Z if ahead == d and ahead < here else d
        remote(
            psend.at[mine_k, :, c], part.at[slot, :, c], p_s.at[d, h], p_r.at[slot, h],
            {"shard": ahead},
        ).start()

    def rounds(r, h):
        @pl.when(z == r)
        def _():
            for d in range(Z - 1, r, -1):
                chain(h, r, d, r + 1, r == 0)

        @pl.when(z == Z - 1 - r)
        def _():
            for d in range(Z - 1 - r):
                chain(h, Z - 1 - r, d, Z - 2 - r, r == 0)

    def store_own(r, n, v):
        own[r:r + n, :] = v

    def weight_grad(i):
        ob_i, ob_t = split(every, i)
        g_i, g_t = split(G, i)
        di = lax.dot_general(ob_i, g_i, TN, preferred_element_type=jnp.float32)
        dt = lax.dot_general(ob_t, g_t, TN, preferred_element_type=jnp.float32)
        return di, dt

    def d_copy(h, n, t):
        return remote(
            dbuf.at[:, rows(t), cols(h, HEAD_DIM)],
            rbuf.at[:, :, cols(s * H + h, HEAD_DIM)],
            d_s.at[h, n], d_r.at[h, n], {"seq": t},
        )

    def backward(h):
        c = cols(h, HEAD_DIM)
        for slot, ok in ((z, z > 0), (Z, z < Z - 1)):

            @pl.when(ok)
            def _():
                remote(
                    part.at[slot, :, c], part.at[slot, :, c],
                    p_s.at[0, h], p_r.at[slot, h], {"shard": imgs[1]},
                ).wait_recv()
                own[:, c] += part[slot, :, c].astype(jnp.float32)

        dout = own[:, c].astype(jnp.bfloat16)
        probs = probs_s[h]
        dprobs = lax.dot_general(dout, heads[2, :, c], NT, preferred_element_type=jnp.float32)
        delta = jnp.sum(dout.astype(jnp.float32) * o_s[:, c], axis=-1, keepdims=True)
        ds = (probs * (dprobs - delta)).astype(jnp.bfloat16)
        dq = jnp.dot(ds, heads[1, :, c], preferred_element_type=jnp.float32) * scale
        dk = lax.dot_general(ds, heads[0, :, c], TN, preferred_element_type=jnp.float32) * scale
        dv = lax.dot_general(
            probs.astype(jnp.bfloat16), dout, TN, preferred_element_type=jnp.float32
        )
        dbuf[0, :, c] = dq.astype(jnp.bfloat16)
        dbuf[1, :, c] = dk.astype(jnp.bfloat16)
        dbuf[2, :, c] = dv.astype(jnp.bfloat16)
        for n, t in ((1, cross), (2, diag), (0, core)):
            d_copy(h, n, t).start()

    half = (H - 1) // 2
    for step in range(H + Z - 1):
        for r in range(Z - 1):
            if 0 <= step - r < H:
                rounds(r, step - r)
        if step == 0:
            gx_wait(z, core, 1)
            gx_wait(z, diag, 2)
            partial(z, store_own)
        if step == 1:
            if Z > 2:
                arrive(1)
                hop(1, lambda c: c.start())
            dw_img[...], dw_txt[...] = weight_grad(z)
        if step >= Z - 1:
            backward(step - Z + 1)
        if step - Z + 1 == half:
            for distance in range(2, Z - 1):
                arrive(distance)
                hop(distance, lambda c: c.start())
    mine_d = pltpu.make_async_copy(dbuf.at[:, rows(s)], rbuf.at[:, :, cols(s, W)], local_sem.at[6])
    mine_d.start()
    for distance in range(max(1, Z - 1), Z):
        arrive(distance)

    def add_image(k, carry):
        di, dt = weight_grad(lax.rem(z + k, Z))
        dw_img[...] += di
        dw_txt[...] += dt
        return carry

    lax.fori_loop(1, Z, add_image, 0)

    mine_d.wait()
    for h in range(H):
        for n, t in enumerate(seqs):
            d_copy(h, n, t).wait_send()
            remote(
                rbuf.at[:, :, cols(t * H + h, HEAD_DIM)],
                rbuf.at[:, :, cols(t * H + h, HEAD_DIM)],
                d_s.at[h, n], d_r.at[h, n], {"seq": t},
            ).wait_recv()
    last = [
        pltpu.make_async_copy(rbuf.at[:, pl.ds(0, text)], out_txt.at[:, 0], local_sem.at[0]),
        pltpu.make_async_copy(rbuf.at[:, pl.ds(text, T - text)], out_img.at[:, 0], local_sem.at[1]),
    ]
    for c in last:
        c.start()
    for c in sends:
        c.wait_send()
    for distance in range(Z - 1):
        hop(distance, lambda c: c.wait_send())
    for k in range(1, Z):
        for h in range(H):
            c = cols(h, HEAD_DIM)
            remote(
                psend.at[k - 1, :, c], part.at[0, :, c],
                p_s.at[imgs[k], h], p_r.at[0, h], {"shard": imgs[k]},
            ).wait_send()
    for c in last:
        c.wait()


def fused(qkv_img, qkv_txt, grad_img, grad_txt, out_w_img, out_w_txt):
    S = lax.axis_size("seq")
    Z = lax.axis_size("shard")
    text = qkv_txt.shape[2]
    T = text + qkv_img.shape[2]
    HDW = qkv_img.shape[3]
    width = grad_img.shape[2]
    W, C = out_w_img.shape
    H = W // HEAD_DIM
    N = S * T
    bf, f4 = jnp.bfloat16, jnp.float32
    V, D = pltpu.VMEM, pltpu.SemaphoreType.DMA
    hbm = pl.BlockSpec(memory_space=pl.ANY)
    vm = pl.BlockSpec(memory_space=pltpu.VMEM)
    return pl.pallas_call(
        functools.partial(fused_kernel, S, Z, text),
        out_shape=(
            jax.ShapeDtypeStruct(qkv_img.shape, bf),
            jax.ShapeDtypeStruct(qkv_txt.shape, bf),
            jax.ShapeDtypeStruct((W, C), f4),
            jax.ShapeDtypeStruct((W, C), f4),
        ),
        in_specs=[hbm, hbm, hbm, hbm, vm, vm],
        out_specs=(hbm, hbm, vm, vm),
        scratch_shapes=[
            V((T, width), bf), V((3, T, HDW), bf), V((3, N, W), bf), V((Z, N, C), bf),
            V((Z - 1, N, W), bf), V((Z + 1, N, W), bf), V((N, W), f4), V((H, N, N), f4),
            V((N, W), f4), V((Z, N, W), bf), V((3, N, W), bf), V((3, T, HDW), bf),
            D((7,)), D((Z,)), D((Z,)), D((Z, 3)), D((Z, 3)), D((S,)), D((S,)),
            D((Z, H)), D((Z + 1, H)), D((Z, 2)), D((Z,)), D((H, 3)), D((H, 3)),
        ],
        compiler_params=pltpu.CompilerParams(
            collective_id=0, has_side_effects=True, vmem_limit_bytes=60 * 1024 * 1024
        ),
    )(qkv_img, qkv_txt, grad_img, grad_txt, out_w_img, out_w_txt)


def local(qkv_img, qkv_txt, grad_img, grad_txt, out_w_img, out_w_txt):
    shard = lax.axis_size("shard")
    weight_rows = 2 * out_w_img.shape[1]
    token_rows = lax.axis_size("seq") * (qkv_img.shape[2] + qkv_txt.shape[2])
    args = (qkv_img, qkv_txt, grad_img, grad_txt, out_w_img, out_w_txt)
    if (
        token_rows <= weight_rows
        and lax.axis_size("seq") == 4
        and lax.axis_size("shard") == 4
        and out_w_img.shape[1] % 128 == 0
        and qkv_txt.shape[2] % 16 == 0
        and qkv_img.shape[2] % 16 == 0
    ):
        return fused(*args)
    if token_rows <= weight_rows:
        return gather_tokens(*args)
    return gather_weights(*args)


def solution(mesh):
    return jax.shard_map(
        local,
        mesh=mesh,
        in_specs=(
            P(None, ("groups", "shard"), "seq", None),
            P(None, ("groups", "shard"), "seq", None),
            P(("groups", "shard"), "seq", None),
            P(("groups", "shard"), "seq", None),
            P("seq", "shard"),
            P("seq", "shard"),
        ),
        out_specs=(
            P(None, ("groups", "shard"), "seq", None),
            P(None, ("groups", "shard"), "seq", None),
            P(("groups", "seq"), "shard"),
            P(("groups", "seq"), "shard"),
        ),
        check_vma=False,
    )
```

```python
import functools

import jax
import jax.numpy as jnp
from jax import lax
from jax.experimental import pallas as pl
from jax.experimental.pallas import tpu as pltpu
from jax.sharding import PartitionSpec as P

HEAD_DIM = 128


def head_backward(query, keys, values, dout):
    scale = HEAD_DIM ** (-0.5)
    scores = jnp.dot(query, keys.T, preferred_element_type=jnp.float32) * scale
    top = jnp.max(scores, axis=-1, keepdims=True)
    expo = jnp.exp(scores - top)
    probs = expo / jnp.sum(expo, axis=-1, keepdims=True)
    probs_low = probs.astype(jnp.bfloat16)
    output = jnp.dot(probs_low, values, preferred_element_type=jnp.float32)
    dprobs = jnp.dot(dout, values.T, preferred_element_type=jnp.float32)
    delta = jnp.sum(dout.astype(jnp.float32) * output, axis=-1, keepdims=True)
    dscore = (probs * (dprobs - delta)).astype(jnp.bfloat16)
    dquery = (jnp.dot(dscore, keys, preferred_element_type=jnp.float32) * scale).astype(
        jnp.bfloat16
    )
    dkeys = (jnp.dot(dscore.T, query, preferred_element_type=jnp.float32) * scale).astype(
        jnp.bfloat16
    )
    dvalues = jnp.dot(probs_low.T, dout, preferred_element_type=jnp.float32).astype(jnp.bfloat16)
    return (output.astype(jnp.bfloat16), dquery, dkeys, dvalues)


def gather_weights(qkv_img, qkv_txt, grad_img, grad_txt, out_w_img, out_w_txt):
    heads_txt, heads_img = (
        lax.all_to_all(qkv_txt, "seq", split_axis=3, concat_axis=2, tiled=True),
        lax.all_to_all(qkv_img, "seq", split_axis=3, concat_axis=2, tiled=True),
    )
    weight_txt, weight_img = (
        lax.all_gather(out_w_txt, "shard", axis=1, tiled=True),
        lax.all_gather(out_w_img, "shard", axis=1, tiled=True),
    )
    full_txt, full_img = (
        lax.all_gather(grad_txt, "seq", axis=1, tiled=True),
        lax.all_gather(grad_img, "seq", axis=1, tiled=True),
    )
    cot_txt = full_txt[0]
    cot_img = full_img[0]
    text_len = cot_txt.shape[0]
    joint = jnp.concatenate([heads_txt[:, 0], heads_img[:, 0]], axis=1)
    total_len = joint.shape[1]
    local_width = joint.shape[2]
    head_count = local_width // HEAD_DIM
    dout = jnp.concatenate(
        [
            jnp.einsum("td,hd->th", cot_txt, weight_txt, preferred_element_type=jnp.float32),
            jnp.einsum("td,hd->th", cot_img, weight_img, preferred_element_type=jnp.float32),
        ],
        axis=0,
    ).astype(jnp.bfloat16)

    def arrange(block):
        return block.reshape(total_len, head_count, HEAD_DIM).transpose(1, 0, 2)

    def restore(block):
        return block.transpose(1, 0, 2).reshape(total_len, local_width)

    results = lax.map(
        lambda items: head_backward(*items),
        (arrange(joint[0]), arrange(joint[1]), arrange(joint[2]), arrange(dout)),
    )
    output = restore(results[0])
    grads = jnp.stack([restore(results[1]), restore(results[2]), restore(results[3])])
    back_txt = grads[:, None, :text_len]
    back_img = grads[:, None, text_len:]
    ret_txt, ret_img = (
        lax.all_to_all(back_txt, "seq", split_axis=2, concat_axis=3, tiled=True),
        lax.all_to_all(back_img, "seq", split_axis=2, concat_axis=3, tiled=True),
    )
    part_txt = jnp.dot(output[:text_len].T, cot_txt, preferred_element_type=jnp.float32)
    part_img = jnp.dot(output[text_len:].T, cot_img, preferred_element_type=jnp.float32)
    sum_txt, sum_img = (
        lax.psum_scatter(
            part_txt.astype(jnp.bfloat16), "shard", scatter_dimension=1, tiled=True
        ).astype(jnp.float32),
        lax.psum_scatter(
            part_img.astype(jnp.bfloat16), "shard", scatter_dimension=1, tiled=True
        ).astype(jnp.float32),
    )
    return (ret_img, ret_txt, sum_img, sum_txt)


def gather_tokens(qkv_img, qkv_txt, grad_img, grad_txt, out_w_img, out_w_txt):
    text = qkv_txt.shape[2]
    tokens = text + qkv_img.shape[2]
    seq = lax.axis_size("seq")
    shard = lax.axis_size("shard")
    grad = jnp.concatenate([grad_txt[0], grad_img[0]], axis=0)
    cols = grad.shape[1] // shard
    grad = lax.all_to_all(
        grad.reshape(tokens, shard, cols).transpose(1, 0, 2), "shard", 0, 0, tiled=True
    )
    joint = jnp.concatenate([qkv_txt[:, 0], qkv_img[:, 0]], axis=1)
    joint = lax.all_to_all(joint, "seq", split_axis=2, concat_axis=1, tiled=True)
    grad = lax.all_gather(grad, "seq", axis=1, tiled=False)
    cot_txt = grad[:, :, :text]
    cot_img = grad[:, :, text:]
    part = jnp.concatenate(
        [
            jnp.einsum("bstd,hd->bsth", cot_txt, out_w_txt, preferred_element_type=jnp.float32),
            jnp.einsum("bstd,hd->bsth", cot_img, out_w_img, preferred_element_type=jnp.float32),
        ],
        axis=2,
    ).astype(jnp.bfloat16)
    part = lax.all_to_all(part, "shard", 0, 0, tiled=True)
    width = joint.shape[2]
    heads = width // HEAD_DIM
    total = seq * tokens
    dout = jnp.sum(part.astype(jnp.float32), axis=0).astype(jnp.bfloat16).reshape(total, width)

    results = []
    for h in range(heads):
        c = slice(h * HEAD_DIM, (h + 1) * HEAD_DIM)
        results.append(head_backward(joint[0, :, c], joint[1, :, c], joint[2, :, c], dout[:, c]))
    output = jnp.concatenate([r[0] for r in results], axis=1)
    every = lax.all_gather(output, "shard", axis=0, tiled=False)
    grads = jnp.stack([jnp.concatenate([r[i] for r in results], axis=1) for i in (1, 2, 3)])
    back = lax.all_to_all(grads, "seq", split_axis=1, concat_axis=2, tiled=True)
    every = every.reshape(shard, seq, tokens, width)
    dw_txt = jnp.einsum(
        "bsth,bstd->hd", every[:, :, :text], cot_txt, preferred_element_type=jnp.float32
    )
    dw_img = jnp.einsum(
        "bsth,bstd->hd", every[:, :, text:], cot_img, preferred_element_type=jnp.float32
    )
    return back[:, None, text:], back[:, None, :text], dw_img, dw_txt


NT = (((1,), (1,)), ((), ()))
TN = (((0,), (0,)), ((), ()))


def fused_kernel(
    S, Z, text, qkv_img, qkv_txt, grad_img, grad_txt, w_img, w_txt,
    out_img, out_txt, dw_img, dw_txt,
    gbuf, qbuf, heads, G, psend, part, own, probs_s, o_s, every, dbuf, rbuf,
    local_sem, gz_s, gz_r, gx_s, gx_r, q_s, q_r, p_s, p_r, o_snd, o_r, d_s, d_r,
):
    T = gbuf.shape[0]
    C = w_img.shape[1]
    W = w_img.shape[0]
    H = W // HEAD_DIM
    s = lax.axis_index("seq")
    z = lax.axis_index("shard")
    core = s + 1 - 2 * lax.rem(s, 2)
    cross = lax.rem(s + 2, S)
    diag = lax.rem(core + 2, S)
    seqs = [core, cross, diag]
    imgs = [lax.rem(z + k, Z) for k in range(Z)]

    def rows(block):
        return pl.ds(pl.multiple_of(block * T, 16), T)

    def cols(block, width):
        if isinstance(block, int):
            return pl.ds(block * width, width)
        return pl.ds(pl.multiple_of(block * width, 128), width)

    stage = [
        pltpu.make_async_copy(grad_txt.at[0], gbuf.at[pl.ds(0, text)], local_sem.at[0]),
        pltpu.make_async_copy(grad_img.at[0], gbuf.at[pl.ds(text, T - text)], local_sem.at[1]),
        pltpu.make_async_copy(qkv_txt.at[:, 0], qbuf.at[:, pl.ds(0, text)], local_sem.at[2]),
        pltpu.make_async_copy(
            qkv_img.at[:, 0], qbuf.at[:, pl.ds(text, T - text)], local_sem.at[3]
        ),
    ]
    for c in stage:
        c.start()
    barrier = pltpu.get_barrier_semaphore()
    for t in seqs:
        pl.semaphore_signal(
            barrier, inc=1, device_id={"seq": t}, device_id_type=pl.DeviceIdType.MESH
        )
    for t in imgs[1:]:
        pl.semaphore_signal(
            barrier, inc=1, device_id={"shard": t}, device_id_type=pl.DeviceIdType.MESH
        )
    pl.semaphore_wait(barrier, S + Z - 2)

    def remote(src, dst, send, recv, where):
        return pltpu.make_async_remote_copy(
            src_ref=src, dst_ref=dst, send_sem=send, recv_sem=recv,
            device_id=where, device_id_type=pl.DeviceIdType.MESH,
        )

    sends = []

    def start(*args):
        c = remote(*args)
        c.start()
        sends.append(c)

    def block(i, t):
        return G.at[i, rows(t)]

    def gx_start(i, t, kind, where):
        start(block(i, t), block(i, t), gx_s.at[i, kind], gx_r.at[i, kind], {"seq": where})

    def gx_wait(i, t, kind):
        remote(
            block(i, t), block(i, t), gx_s.at[i, kind], gx_r.at[i, kind], {"seq": core}
        ).wait_recv()

    stage[0].wait()
    stage[1].wait()
    for k in range(1, Z):
        i = imgs[k]
        start(gbuf.at[:, cols(i, C)], block(z, s), gz_s.at[k], gz_r.at[z], {"shard": i})
    mine = pltpu.make_async_copy(gbuf.at[:, cols(z, C)], block(z, s), local_sem.at[4])
    mine.start()
    mine.wait()
    gx_start(z, s, 0, cross)
    gx_start(z, s, 1, core)
    stage[2].wait()
    stage[3].wait()
    for n, t in enumerate((cross, diag, core)):
        start(qbuf.at[:, :, cols(t, W)], heads.at[:, rows(s)], q_s.at[n], q_r.at[s], {"seq": t})
    mine_q = pltpu.make_async_copy(qbuf.at[:, :, cols(s, W)], heads.at[:, rows(s)], local_sem.at[5])
    mine_q.start()

    def split(ref, i):
        image = jnp.concatenate([ref[i, t * T + text:(t + 1) * T, :] for t in range(S)], axis=0)
        words = jnp.concatenate([ref[i, t * T:t * T + text, :] for t in range(S)], axis=0)
        return image, words

    def partial(i, store):
        image, words = split(G, i)
        pi = lax.dot_general(image, w_img[...], NT, preferred_element_type=jnp.float32)
        pt = lax.dot_general(words, w_txt[...], NT, preferred_element_type=jnp.float32)
        n = T - text
        for t in range(S):
            store(t * T, text, pt[t * text:(t + 1) * text])
            store(t * T + text, n, pi[t * n:(t + 1) * n])

    def relay(k):
        gx_wait(imgs[k], cross, 0)
        gx_start(imgs[k], cross, 2, core)

    def produce(k):
        i = imgs[k]
        gx_wait(i, core, 1)
        gx_wait(i, diag, 2)

        def store(r, n, v):
            psend[k - 1, r:r + n, :] = v.astype(jnp.bfloat16)

        partial(i, store)

    scale = HEAD_DIM ** (-0.5)

    def forward(h, carry):
        c = cols(h, HEAD_DIM)
        scores = lax.dot_general(
            heads[0, :, c], heads[1, :, c], NT, preferred_element_type=jnp.float32
        ) * scale
        expo = jnp.exp(scores - jnp.max(scores, axis=-1, keepdims=True))
        probs = expo * (1.0 / jnp.sum(expo, axis=-1, keepdims=True))
        probs_s[h] = probs
        o = jnp.dot(probs.astype(jnp.bfloat16), heads[2, :, c], preferred_element_type=jnp.float32)
        o_s[:, c] = o
        every[z, :, c] = o.astype(jnp.bfloat16)
        return carry

    for k in range(1, Z):
        i = imgs[k]
        remote(block(i, s), block(i, s), gz_s.at[k], gz_r.at[i], {"shard": i}).wait_recv()
        gx_start(i, s, 0, cross)
        gx_start(i, s, 1, core)
    mine_q.wait()
    for t in seqs:
        remote(
            heads.at[:, rows(t)], heads.at[:, rows(t)], q_s.at[0], q_r.at[t], {"seq": t}
        ).wait_recv()

    def o_copy(j, way, to):
        return remote(every.at[j], every.at[j], o_snd.at[j, way], o_r.at[j], {"shard": to})

    def hop(distance, act):
        left, right = z - distance, z + distance

        @pl.when((left >= 0) & (z < Z - 1))
        def _():
            act(o_copy(left, 0, z + 1))

        @pl.when((right < Z) & (z > 0))
        def _():
            act(o_copy(right, 1, z - 1))

    def arrive(distance):
        for j, ok in ((z - distance, z >= distance), (z + distance, z + distance < Z)):

            @pl.when(ok)
            def _():
                remote(every.at[j], every.at[j], o_snd.at[j, 0], o_r.at[j], {"shard": imgs[1]}).wait_recv()

    per = -(-H // Z)
    for k in range(Z):
        lax.fori_loop(min(H, k * per), min(H, (k + 1) * per), forward, 0)
        if k < Z - 1:
            relay(k)
    hop(0, lambda c: c.start())
    for k in range(1, Z - 1):
        produce(k)
    relay(Z - 1)
    produce(Z - 1)

    def chain(h, here, d, ahead, first):
        c = cols(h, HEAD_DIM)
        mine_k = (d - here) % Z - 1
        if not first:
            remote(
                part.at[d, :, c], part.at[d, :, c], p_s.at[d, h], p_r.at[d, h], {"shard": ahead}
            ).wait_recv()
            psend[mine_k, :, c] = (
                psend[mine_k, :, c].astype(jnp.float32) + part[d, :, c].astype(jnp.float32)
            ).astype(jnp.bfloat16)
        slot = Z if ahead == d and ahead < here else d
        remote(
            psend.at[mine_k, :, c], part.at[slot, :, c], p_s.at[d, h], p_r.at[slot, h],
            {"shard": ahead},
        ).start()

    def rounds(r, h):
        @pl.when(z == r)
        def _():
            for d in range(Z - 1, r, -1):
                chain(h, r, d, r + 1, r == 0)

        @pl.when(z == Z - 1 - r)
        def _():
            for d in range(Z - 1 - r):
                chain(h, Z - 1 - r, d, Z - 2 - r, r == 0)

    def store_own(r, n, v):
        own[r:r + n, :] = v

    def weight_grad(i):
        ob_i, ob_t = split(every, i)
        g_i, g_t = split(G, i)
        di = lax.dot_general(ob_i, g_i, TN, preferred_element_type=jnp.float32)
        dt = lax.dot_general(ob_t, g_t, TN, preferred_element_type=jnp.float32)
        return di, dt

    def d_copy(h, n, t):
        return remote(
            dbuf.at[:, rows(t), cols(h, HEAD_DIM)],
            rbuf.at[:, :, cols(s * H + h, HEAD_DIM)],
            d_s.at[h, n], d_r.at[h, n], {"seq": t},
        )

    def backward(h):
        c = cols(h, HEAD_DIM)
        for slot, ok in ((z, z > 0), (Z, z < Z - 1)):

            @pl.when(ok)
            def _():
                remote(
                    part.at[slot, :, c], part.at[slot, :, c],
                    p_s.at[0, h], p_r.at[slot, h], {"shard": imgs[1]},
                ).wait_recv()
                own[:, c] += part[slot, :, c].astype(jnp.float32)

        dout = own[:, c].astype(jnp.bfloat16)
        probs = probs_s[h]
        dprobs = lax.dot_general(dout, heads[2, :, c], NT, preferred_element_type=jnp.float32)
        delta = jnp.sum(dout.astype(jnp.float32) * o_s[:, c], axis=-1, keepdims=True)
        ds = (probs * (dprobs - delta)).astype(jnp.bfloat16)
        dq = jnp.dot(ds, heads[1, :, c], preferred_element_type=jnp.float32) * scale
        dk = lax.dot_general(ds, heads[0, :, c], TN, preferred_element_type=jnp.float32) * scale
        dv = lax.dot_general(
            probs.astype(jnp.bfloat16), dout, TN, preferred_element_type=jnp.float32
        )
        dbuf[0, :, c] = dq.astype(jnp.bfloat16)
        dbuf[1, :, c] = dk.astype(jnp.bfloat16)
        dbuf[2, :, c] = dv.astype(jnp.bfloat16)
        for n, t in ((1, cross), (2, diag), (0, core)):
            d_copy(h, n, t).start()

    half = (H - 1) // 2
    for step in range(H + Z - 1):
        for r in range(Z - 1):
            if 0 <= step - r < H:
                rounds(r, step - r)
        if step == 0:
            gx_wait(z, core, 1)
            gx_wait(z, diag, 2)
            partial(z, store_own)
        if step == 1:
            if Z > 2:
                arrive(1)
                hop(1, lambda c: c.start())
            dw_img[...], dw_txt[...] = weight_grad(z)
        if step >= Z - 1:
            backward(step - Z + 1)
        if step - Z + 1 == half:
            for distance in range(2, Z - 1):
                arrive(distance)
                hop(distance, lambda c: c.start())
    mine_d = pltpu.make_async_copy(dbuf.at[:, rows(s)], rbuf.at[:, :, cols(s, W)], local_sem.at[6])
    mine_d.start()
    for distance in range(max(1, Z - 1), Z):
        arrive(distance)

    def add_image(k, carry):
        di, dt = weight_grad(lax.rem(z + k, Z))
        dw_img[...] += di
        dw_txt[...] += dt
        return carry

    lax.fori_loop(1, Z, add_image, 0)

    mine_d.wait()
    for h in range(H):
        for n, t in enumerate(seqs):
            d_copy(h, n, t).wait_send()
            remote(
                rbuf.at[:, :, cols(t * H + h, HEAD_DIM)],
                rbuf.at[:, :, cols(t * H + h, HEAD_DIM)],
                d_s.at[h, n], d_r.at[h, n], {"seq": t},
            ).wait_recv()
    last = [
        pltpu.make_async_copy(rbuf.at[:, pl.ds(0, text)], out_txt.at[:, 0], local_sem.at[0]),
        pltpu.make_async_copy(rbuf.at[:, pl.ds(text, T - text)], out_img.at[:, 0], local_sem.at[1]),
    ]
    for c in last:
        c.start()
    for c in sends:
        c.wait_send()
    for distance in range(Z - 1):
        hop(distance, lambda c: c.wait_send())
    for k in range(1, Z):
        for h in range(H):
            c = cols(h, HEAD_DIM)
            remote(
                psend.at[k - 1, :, c], part.at[0, :, c],
                p_s.at[imgs[k], h], p_r.at[0, h], {"shard": imgs[k]},
            ).wait_send()
    for c in last:
        c.wait()


def fused(qkv_img, qkv_txt, grad_img, grad_txt, out_w_img, out_w_txt):
    S = lax.axis_size("seq")
    Z = lax.axis_size("shard")
    text = qkv_txt.shape[2]
    T = text + qkv_img.shape[2]
    HDW = qkv_img.shape[3]
    width = grad_img.shape[2]
    W, C = out_w_img.shape
    H = W // HEAD_DIM
    N = S * T
    bf, f4 = jnp.bfloat16, jnp.float32
    V, D = pltpu.VMEM, pltpu.SemaphoreType.DMA
    hbm = pl.BlockSpec(memory_space=pl.ANY)
    vm = pl.BlockSpec(memory_space=pltpu.VMEM)
    return pl.pallas_call(
        functools.partial(fused_kernel, S, Z, text),
        out_shape=(
            jax.ShapeDtypeStruct(qkv_img.shape, bf),
            jax.ShapeDtypeStruct(qkv_txt.shape, bf),
            jax.ShapeDtypeStruct((W, C), f4),
            jax.ShapeDtypeStruct((W, C), f4),
        ),
        in_specs=[hbm, hbm, hbm, hbm, vm, vm],
        out_specs=(hbm, hbm, vm, vm),
        scratch_shapes=[
            V((T, width), bf), V((3, T, HDW), bf), V((3, N, W), bf), V((Z, N, C), bf),
            V((Z - 1, N, W), bf), V((Z + 1, N, W), bf), V((N, W), f4), V((H, N, N), f4),
            V((N, W), f4), V((Z, N, W), bf), V((3, N, W), bf), V((3, T, HDW), bf),
            D((7,)), D((Z,)), D((Z,)), D((Z, 3)), D((Z, 3)), D((S,)), D((S,)),
            D((Z, H)), D((Z + 1, H)), D((Z, 2)), D((Z,)), D((H, 3)), D((H, 3)),
        ],
        compiler_params=pltpu.CompilerParams(
            collective_id=0, has_side_effects=True, vmem_limit_bytes=60 * 1024 * 1024
        ),
    )(qkv_img, qkv_txt, grad_img, grad_txt, out_w_img, out_w_txt)


def local(qkv_img, qkv_txt, grad_img, grad_txt, out_w_img, out_w_txt):
    shard = lax.axis_size("shard")
    weight_rows = 2 * out_w_img.shape[1]
    token_rows = lax.axis_size("seq") * (qkv_img.shape[2] + qkv_txt.shape[2])
    args = (qkv_img, qkv_txt, grad_img, grad_txt, out_w_img, out_w_txt)
    if (
        token_rows <= weight_rows
        and lax.axis_size("seq") == 4
        and lax.axis_size("shard") == 4
        and out_w_img.shape[1] % 128 == 0
        and qkv_txt.shape[2] % 16 == 0
        and qkv_img.shape[2] % 16 == 0
    ):
        return fused(*args)
    if token_rows <= weight_rows:
        return gather_tokens(*args)
    return gather_weights(*args)


def solution(mesh):
    return jax.shard_map(
        local,
        mesh=mesh,
        in_specs=(
            P(None, ("groups", "shard"), "seq", None),
            P(None, ("groups", "shard"), "seq", None),
            P(("groups", "shard"), "seq", None),
            P(("groups", "shard"), "seq", None),
            P("seq", "shard"),
            P("seq", "shard"),
        ),
        out_specs=(
            P(None, ("groups", "shard"), "seq", None),
            P(None, ("groups", "shard"), "seq", None),
            P(("groups", "seq"), "shard"),
            P(("groups", "seq"), "shard"),
        ),
        check_vma=False,
    )
```
